512 devices in a mesh: lat: 32 (over y, x, core), lon: 16 (over z).
Axes of the slice: x: 4, y: 4, z: 16, core: 2. Of those that a mesh axis runs over, the one named last changes fastest.
Arguments:
- grid_fields: bfloat16 [32, 1280, 2560], P(None, 'lat', 'lon'), may hold values from -6 to 6
- weight_in: bfloat16 [32, 256], replicated, may hold values from -1 to 1
- weight_out: bfloat16 [256, 32], replicated, may hold values from -0.375 to 0.375
- legendre_basis: bfloat16 [1280, 640, 640], P('lat', 'lon'), may hold values from -0.15625 to 0.15625
- block_slot: int32 [80], replicated, may hold values from 0 to 79, each once
- spectrum_grad: bfloat16 [640, 640, 64], P('lat', 'lon'), may hold values from -6 to 6
Outputs:
- spectrum: float32 [640, 640, 64], P('lat', 'lon')
- fields_grad: bfloat16 [32, 1280, 2560], P(None, 'lat', 'lon')
The draws below stay inside these ranges and needn't reach their ends.
Inputs may be any that keep to these rules, and one draw needn't show every extreme that they name: block_slot names every slot block once.
All inputs are finite; a program needn't handle non-finite values.
Results may differ from the reference program's by a relative error of at most 0.019.
Values may be sent and summed in bfloat16 or wider, within the bound.
No kernel may reach another device: no remote copies, remote signals or barrier semaphores. Data moves between devices by JAX's collectives and lax.ppermute only.
A program may use at most 128 MiB of HBM per device.

```python
import math
import jax
import jax.numpy as jnp
from jax import lax

C = 32
HIDDEN_SIZE = 256
NLAT = 1280
NLON = 2560
M = 640
NDEG = 640
MB = 8
MBLK = 80
N_LAT = 32


def level_of(stream_key, dims, shards, smallest, top_value):
    factor_of, own = 1.0, jax.random.fold_in(stream_key, 6)
    for axis_at, parts in shards:
        steps = jnp.exp(jax.random.uniform(jax.random.fold_in(own, axis_at), (parts,), jnp.float32, smallest / len(shards), top_value / len(shards)))
        factor_of = factor_of * jnp.repeat(steps, dims[axis_at] // parts).reshape([-1 if axis == axis_at else 1 for axis in range(len(dims))])
    return factor_of


def centred(rng, shape, spread, bound, pieces=(), held_as=jnp.bfloat16):
    values = spread * jax.random.normal(rng, shape, jnp.float32)
    if pieces:
        values = values * level_of(rng, shape, pieces, -0.22, 0.18)
    return jnp.clip(values, -bound, bound).astype(held_as)


def setup_inputs(seed: int = 0) -> dict:
    arg_keys = jax.random.split(jax.random.key(seed), 7)
    return {
        "grid_fields": centred(arg_keys[0], (C, NLAT, NLON), 1.0, 6.0, ((1, 32), (2, 16))),
        "weight_in": centred(arg_keys[1], (C, HIDDEN_SIZE), C ** -0.5, 1.0),
        "weight_out": centred(arg_keys[2], (HIDDEN_SIZE, C), HIDDEN_SIZE ** -0.5, 0.375),
        "legendre_basis": centred(arg_keys[3], (NLAT, M, NDEG), NLAT ** -0.5, 0.15625, ((0, 32), (1, 16))),
        "block_slot": jax.random.permutation(arg_keys[4], MBLK).astype(jnp.int32),
        "spectrum_grad": centred(arg_keys[5], (NDEG, M, 2 * C), 1.0, 6.0, ((0, 32), (1, 16))),
    }


HIGH = lax.Precision.HIGHEST

def slot_waves(block_slot):
    blocks = block_slot.shape[0]
    width = M // blocks
    slots = jnp.arange(blocks, dtype=jnp.int32)
    match = block_slot[None, :] == slots[:, None]
    holder = lax.optimization_barrier(jnp.sum(jnp.where(match, slots[None, :], 0), axis=1)).astype(jnp.int32)
    positions = jnp.arange(M, dtype=jnp.int32)
    return (holder[positions // width] * width + positions % width).astype(jnp.int32)

def dft_table(waves):
    longitude = jnp.arange(NLON, dtype=jnp.int32)
    phase = longitude[:, None] * waves[None, :] % NLON
    angle = phase.astype(jnp.float32) * (2.0 * math.pi / NLON)
    factor = 1.0 / math.sqrt(NLON)
    table = jnp.stack((jnp.cos(angle) * factor, -jnp.sin(angle) * factor), axis=-1)
    return table.reshape(NLON, 2 * M).astype(jnp.bfloat16)

def degree_keep(waves, first, count):
    degrees = first + jnp.arange(count, dtype=jnp.int32)
    return degrees[None, :] + waves[:, None] <= M - 1

def rounded(values):
    return lax.optimization_barrier(values.astype(jnp.bfloat16)).astype(jnp.float32)

def reference(grid_fields, weight_in, weight_out, legendre_basis, block_slot, spectrum_grad):
    lat_group = NLAT // N_LAT
    waves = slot_waves(block_slot)
    table = dft_table(waves).astype(jnp.float32)
    inward = weight_in.astype(jnp.float32)
    outward = weight_out.astype(jnp.float32)

    def column_step(fields):
        values = fields.reshape(C, -1).astype(jnp.float32)
        hidden_pre = jnp.dot(inward.T, values, precision=HIGH)
        active = rounded(jax.nn.silu(hidden_pre))
        mixed = values + jnp.dot(outward.T, active, precision=HIGH)
        return mixed.astype(jnp.bfloat16).reshape(fields.shape)
    grouped = jnp.transpose(grid_fields.reshape(C, N_LAT, lat_group, NLON), (1, 0, 2, 3))
    columns = lax.map(column_step, grouped)
    fourier = jnp.dot(columns.reshape(-1, NLON).astype(jnp.float32), table, precision=HIGH)
    fourier = fourier.astype(jnp.bfloat16).reshape(N_LAT, C, lat_group, M, 2)
    keep = degree_keep(waves, 0, NDEG).astype(jnp.float32)

    def basis_block(index):
        start = index * MB
        block = lax.dynamic_slice_in_dim(legendre_basis, start, MB, 1).astype(jnp.float32)
        mask_block = lax.dynamic_slice_in_dim(keep, start, MB, 0)
        return block * mask_block[None]

    def forward_block(index):
        block = basis_block(index).reshape(N_LAT, lat_group, MB, NDEG)
        data = lax.dynamic_slice_in_dim(fourier, index * MB, MB, 3).astype(jnp.float32)
        partial_sums = jnp.einsum('glsj,gclsr->gjsrc', block, data, precision=HIGH)
        return lax.optimization_barrier(jnp.sum(rounded(partial_sums), axis=0))
    indices = jnp.arange(MBLK, dtype=jnp.int32)
    spectral = lax.map(forward_block, indices)
    spectrum = jnp.transpose(spectral, (1, 0, 2, 3, 4)).reshape(NDEG, M, 2 * C)

    def backward_block(index):
        block = basis_block(index)
        seeds = lax.dynamic_slice_in_dim(spectrum_grad, index * MB, MB, 1).astype(jnp.float32)
        seeds = seeds.reshape(NDEG, MB, 2, C)
        return jnp.einsum('lsj,jsrc->clsr', block, seeds, precision=HIGH).astype(jnp.bfloat16)
    gradients = lax.map(backward_block, indices)
    fourier_grad = jnp.transpose(gradients, (1, 2, 0, 3, 4)).reshape(C, NLAT, 2 * M)
    column_grad = jnp.dot(fourier_grad.reshape(-1, 2 * M).astype(jnp.float32), table.T, precision=HIGH)
    column_grad = column_grad.astype(jnp.bfloat16).reshape(C, NLAT, NLON)

    def column_back(pair):
        fields, seeds = pair
        values = fields.reshape(C, -1).astype(jnp.float32)
        hidden_pre = jnp.dot(inward.T, values, precision=HIGH)
        upstream = seeds.reshape(C, -1).astype(jnp.float32)
        act_grad = jnp.dot(outward, upstream, precision=HIGH)
        sigma = jax.nn.sigmoid(hidden_pre)
        pre_grad = rounded(act_grad * sigma * (1.0 + hidden_pre * (1.0 - sigma)))
        result = upstream + jnp.dot(inward, pre_grad, precision=HIGH)
        return result.astype(jnp.bfloat16).reshape(fields.shape)
    seeds_grouped = jnp.transpose(column_grad.reshape(C, N_LAT, lat_group, NLON), (1, 0, 2, 3))
    backed = lax.map(column_back, (grouped, seeds_grouped))
    fields_grad = jnp.transpose(backed, (1, 0, 2, 3)).reshape(C, NLAT, NLON)
    return (spectrum, fields_grad)
```

```python
import math

import jax
import jax.numpy as jnp
import numpy as np
from jax import lax
from jax.experimental import pallas as pl
from jax.experimental.pallas import tpu as pltpu
from jax.sharding import Mesh
from jax.sharding import PartitionSpec as P

NLON = 2560
M = 640
F32 = jnp.float32
BF16 = jnp.bfloat16

C = 32
H = 256
L = 40
K = 160
Z = 16
S = 40
J = 640
JD = 20
SP = S // 2
BB = 5
NB = 80
GR = 104
WR = 56
JW = 32 * 24
VMEM = 60 * 1024 * 1024


def dot(a, b, da, db):
    return lax.dot_general(a, b, (((da,), (db,)), ((), ())), preferred_element_type=F32)


def lanes(rows):
    return lax.broadcasted_iota(jnp.int32, (rows, 128), 1)


def grid_row(c2, t):
    return c2 * 40 + t if t < 40 else 80 + c2 * 10 + t - 40


def wave_piece(q, c2):
    if c2 == 0:
        return (q, 0) if q < 56 else (q - 24, 1)
    return (q, 1) if q < 32 else (q - 32, 2)


def row_pieces(row):
    first = (row, 0)
    second = (row, 1) if row < 32 else (row + 24, 0)
    third = (row + 32, 1) if row < 48 else None
    return first, second, third


def slot_q(s, r):
    return (s % 8 * 2 + r) * BB + s // 8


def roll(v, shift):
    shift = shift % 128
    return v if shift == 0 else pltpu.roll(v, shift, 1)


def call(kernel, name, out_shape, scratch, smem=0, hbm=(), out_hbm=False):
    def run(*args):
        specs = [
            pl.BlockSpec(memory_space=pltpu.SMEM if i < smem else pl.ANY if i in hbm else pltpu.VMEM)
            for i in range(len(args))
        ]
        one = not isinstance(out_shape, (tuple, list))
        outs = pl.BlockSpec(memory_space=pl.ANY if out_hbm else pltpu.VMEM)
        return pl.pallas_call(
            kernel,
            name=name,
            out_shape=out_shape,
            in_specs=specs,
            out_specs=outs if one else tuple(outs for _ in out_shape),
            scratch_shapes=scratch,
            compiler_params=pltpu.CompilerParams(vmem_limit_bytes=VMEM),
            cost_estimate=pl.CostEstimate(flops=1_000_000, bytes_accessed=100_000, transcendentals=0),
        )(*args)

    return run


def shape(dims, dtype=BF16):
    return jax.ShapeDtypeStruct(dims, dtype)


def prep_basis_kernel(own_ref, basis_ref, masked_ref, turned_ref, bs, tmp, column, wide):
    for row in range(L):
        v = basis_ref[row].astype(F32)
        for t in range(5):
            bs[t, row * S : (row + 1) * S, :] = v[:, 128 * t : 128 * t + 128]
    tmp[...] = jnp.zeros_like(tmp)
    wide[...] = jnp.zeros_like(wide)
    lane = lanes(L)

    def two_pairs(g, carry):
        for odd in range(2):
            p = 2 * g + odd
            for t in range(5):
                for e in range(2):
                    s = 2 * p + e
                    wave = own_ref[s // 8] * 8 + s % 8
                    v = bs[t, pl.ds(s, L, stride=S), :]
                    tmp[odd, t, 64 * e : 64 * e + L, :] = jnp.where(lane + 128 * t + wave <= M - 1, v, 0.0)
                column[odd, 128 * t : 128 * t + 128, :] = tmp[odd, t].T
            for n in range(32):
                at = 24 * n + 4 * odd
                wide[odd, at : at + JD, :] = column[odd, JD * n : JD * n + JD, :]
            turned_ref[p] = wide[odd].astype(BF16)
            for t in range(6):
                v = wide[odd, 128 * t : 128 * t + 128, :].T
                both = jnp.concatenate([v[0:L], v[64 : 64 + L]], axis=0).astype(BF16)
                masked_ref[p, :, 128 * t : 128 * t + 128] = both
        return carry

    lax.fori_loop(0, SP // 2, two_pairs, 0)


def prep_table_kernel(cb_ref, sb_ref, ci_ref, si_ref, table_ref):
    low = lanes(NB) < 64

    def angle(i, t):
        cb, sb = cb_ref[:, 128 * t : 128 * t + 128], sb_ref[:, 128 * t : 128 * t + 128]
        ci, si = ci_ref[i : i + 1, 128 * t : 128 * t + 128], si_ref[i : i + 1, 128 * t : 128 * t + 128]
        return cb * ci - sb * si, sb * ci + cb * si

    for p in range(4):
        for m, i in enumerate((p, 8 - p) if p else (0, 4)):
            for t in range(3):
                c, s = angle(i, t)
                zero = jnp.zeros_like(c)
                if p == 0:
                    first, second = (c, -s), (zero, zero)
                    if m == 1:
                        first, second = second, first
                elif m == 0:
                    first, second = (c, -s), (s, c)
                else:
                    first, second = (c, -s), (-s, -c)
                for r in range(2):
                    rows = slice((m * 2 + r) * NB, (m * 2 + r + 1) * NB)
                    if t < 2:
                        table_ref[p, rows, 128 * t : 128 * t + 128] = first[r].astype(BF16)
                        table_ref[p, rows, 256 + 128 * t : 384 + 128 * t] = second[r].astype(BF16)
                    else:
                        both = jnp.where(low, first[r], second[r])
                        table_ref[p, rows, 512:640] = both.astype(BF16)


def column_kernel(x_ref, win_ref, wout_ref, out_ref, keep_ref, main, rest, out):
    for c in range(C):
        v = x_ref[c].astype(F32)
        main[c * L : (c + 1) * L, :] = v[:, :128]
        rest[c * L : (c + 1) * L, 0:32] = v[:, 128:K]
    lane = lanes(C)
    for t in range(50):
        if t < 40:
            v = main[pl.ds(t, C, stride=L), :]
        else:
            v = rest[pl.ds(t - 40, C, stride=L), :]
            for e in range(1, 4):
                v = jnp.where(lane >= 32 * e, roll(rest[pl.ds(t - 40 + 10 * e, C, stride=L), :], 32 * e), v)
        keep_ref[:, 128 * t : 128 * t + 128] = v.astype(BF16)
    win, wout = win_ref[...], wout_ref[...]
    for chunk in range(10):
        x = keep_ref[:, 640 * chunk : 640 * chunk + 640]
        pre = dot(win, x, 0, 0)
        half = 0.5 * pre
        active = (half + half * jnp.tanh(half)).astype(BF16)
        y = x.astype(F32) + dot(wout, active, 1, 0)
        for k in range(5):
            for c2 in range(2):
                row = grid_row(c2, 5 * chunk + k)
                out[pl.ds(row, Z, stride=GR), :] = y[Z * c2 : Z * c2 + Z, 128 * k : 128 * k + 128]
    for d in range(Z):
        out_ref[d] = out[d * GR : (d + 1) * GR, :].astype(BF16)


def column_back_kernel(keep_ref, g_ref, win_ref, wout_ref, out_ref, main, rest, got, up):
    for d in range(Z):
        got[d * GR : (d + 1) * GR, :] = g_ref[d].astype(F32)
    win, wout = win_ref[...], wout_ref[...]
    for chunk in range(10):
        for k in range(5):
            t = 5 * chunk + k
            for c2 in range(2):
                up[Z * c2 : Z * c2 + Z, 128 * k : 128 * k + 128] = got[pl.ds(grid_row(c2, t), Z, stride=GR), :]
        x = keep_ref[:, 640 * chunk : 640 * chunk + 640]
        upstream = up[...]
        pre = dot(win, x, 0, 0)
        act_grad = dot(wout, upstream.astype(BF16), 0, 0)
        sigma = 0.5 + 0.5 * jnp.tanh(0.5 * pre)
        pre_grad = (act_grad * sigma * (1.0 + pre * (1.0 - sigma))).astype(BF16)
        y = upstream + dot(win, pre_grad, 1, 0)
        for k in range(5):
            t = 5 * chunk + k
            v = y[:, 128 * k : 128 * k + 128]
            if t < 40:
                main[pl.ds(t, C, stride=L), :] = v
            else:
                for e in range(4):
                    rest[pl.ds(t - 40 + 10 * e, C, stride=L), :] = roll(v, -32 * e)
    for c in range(C):
        out_ref[c, :, 0:128] = main[c * L : (c + 1) * L, :].astype(BF16)
        out_ref[c, :, 128:K] = rest[c * L : (c + 1) * L, 0:32].astype(BF16)


def eight(x):
    root = math.sqrt(0.5)
    s = [x[p] + x[p + 4] for p in range(4)]
    d = [x[p] - x[p + 4] for p in range(4)]
    e0, e1, o0, o1 = s[0] + s[2], s[0] - s[2], s[1] + s[3], s[1] - s[3]
    u, v = root * (d[1] - d[3]), root * (d[1] + d[3])
    return [(e0 + o0, e0 - o0), (d[0] + u, -d[2] - v), (e1, -o1), (d[0] - u, d[2] - v)]


def eight_back(pairs):
    root = math.sqrt(0.5)
    (a0, b0), (a1, b1), (a2, b2), (a3, b3) = pairs
    plus, minus = a0 + b0, a0 - b0
    sa, da, sb, db = a1 + a3, a1 - a3, b1 + b3, b1 - b3
    even0, even2 = plus + a2, plus - a2
    odd1, odd3 = minus - b2, minus + b2
    u, v = root * da, root * sb
    return [
        even0 + sa,
        odd1 + (u - v),
        even2 - db,
        odd3 - (u + v),
        even0 - sa,
        odd1 - (u - v),
        even2 + db,
        odd3 + (u + v),
    ]


def fourier_kernel(in_ref, table_ref, out_ref, got, low, waves, out):
    for d in range(Z):
        got[d * GR : (d + 1) * GR, :] = in_ref[d].astype(F32)
    lane = lanes(20)
    mains = [[], []]
    packed = [[], []]
    for h in range(2):
        mains[h] = eight([got[(2 * p + h) * GR : (2 * p + h) * GR + 80, :] for p in range(8)])
        packed[h] = eight([got[(2 * p + h) * GR + 80 : (2 * p + h) * GR + 100, :] for p in range(8)])
    for i in range(4):
        parts = [packed[pos % 2][i][pos // 2] for pos in range(4)]
        for e in range(4):
            v = roll(parts[0], -32 * e)
            for pos in range(1, 4):
                v = jnp.where(lane >= 32 * pos, roll(parts[pos], 32 * (pos - e)), v)
            low[10 * e : 10 * e + 10, :] = v[0:10]
            low[40 + 10 * e : 50 + 10 * e, :] = v[10:20]
        left = jnp.concatenate(
            [mains[0][i][0], mains[1][i][0], mains[0][i][1], mains[1][i][1], low[0:80, :]], axis=1
        ).astype(BF16)
        left = jnp.concatenate([left, jnp.zeros((48, 640), BF16)], axis=0)
        result = dot(table_ref[i], left, 1, 1)
        for m, w in enumerate((i, 8 - i) if i else (0, 4)):
            waves[w * 160 : w * 160 + 160, :] = result[m * 160 : m * 160 + 160]
    pack_waves(waves, lambda q: q * Z, out, out_ref)


def pack_waves(waves, row_of, out, out_ref):
    lane = lanes(Z)
    for row in range(WR):
        first, second, third = row_pieces(row)
        v = waves[pl.ds(row_of(first[0]), Z), :]
        if second[1] == 0:
            v = jnp.where(lane >= 40, roll(waves[pl.ds(row_of(second[0]), Z), :], 40), v)
        if third is not None:
            v = jnp.where(lane >= 80, roll(waves[pl.ds(row_of(third[0]), Z), :], 40), v)
        out[pl.ds(row, Z, stride=WR), :] = v
    for d in range(Z):
        out_ref[d] = out[d * WR : (d + 1) * WR, :].astype(BF16)


def legendre_kernel(core_ref, in_ref, turned_hbm, mine_hbm, other_hbm, got, block, out, turned, mine, other, come, go):
    copies = [
        pltpu.make_async_copy(turned_hbm.at[pl.ds(2 * g, 2)], turned.at[pl.ds(2 * g, 2)], come.at[g])
        for g in range(S // 4)
    ]
    for copy in copies:
        copy.start()
    for d in range(Z):
        got[d * WR : (d + 1) * WR, :] = in_ref[d].astype(F32)
    lane = lanes(Z)
    for g in range(S // 4):
        block[g, 0:128, 128:256] = jnp.zeros((128, 128), BF16)
        block[g, 128:256, 0:128] = jnp.zeros((128, 128), BF16)
        for s4 in range(4):
            off, tile = 64 * (s4 % 2), s4 // 2
            for r in range(2):
                for c2 in range(2):
                    row, place = wave_piece(slot_q(4 * g + s4, r), c2)
                    v = roll(got[pl.ds(row, Z, stride=WR), :], off - 40 * place)
                    v = jnp.where((lane >= off) & (lane < off + L), v, 0.0).astype(BF16)
                    at = s4 * 64 + r * 32 + c2 * Z
                    block[g, at : at + Z, 128 * tile : 128 * tile + 128] = v
    for g in range(S // 4):
        copies[g].wait()
        left = jnp.concatenate([turned[2 * g], turned[2 * g + 1]], axis=1)
        result = dot(left, block[g], 1, 1)
        for n in range(32):
            even, odd = result[24 * n : 24 * n + 24, 0:128], result[24 * n : 24 * n + 24, 128:256]
            at = n * 400 + g * 40
            out[at : at + 16, :] = even[0:16]
            out[at + 16 : at + 24, :] = even[16:24] + odd[0:8]
            out[at + 24 : at + 40, :] = odd[8:24]
    core = core_ref[0]
    copies = []
    for n in range(16):
        rows = pl.ds(n * 400, 400)
        chip = n % 4 * 4 + n // 4
        mine[rows, :] = out[pl.ds(pl.multiple_of((2 * chip + core) * 400, 16), 400), :].astype(BF16)
        other[rows, :] = out[pl.ds(pl.multiple_of((2 * chip + 1 - core) * 400, 16), 400), :].astype(BF16)
        if n % 4 == 3:
            part = pl.ds((n - 3) * 400, 1600)
            copies.append(pltpu.make_async_copy(mine.at[part], mine_hbm.at[part], go.at[n // 4]))
            copies.append(pltpu.make_async_copy(other.at[part], other_hbm.at[part], go.at[4 + n // 4]))
            copies[-2].start()
            copies[-1].start()
    for copy in copies:
        copy.wait()


def core_sum_kernel(mine_ref, other_ref, out_ref):
    for n in range(16):
        rows = pl.ds(n * 400, 400)
        out_ref[rows, :] = (mine_ref[rows, :].astype(F32) + other_ref[rows, :].astype(F32)).astype(BF16)


def parts_kernel(place_ref, in_ref, *out_refs):
    for d, out_ref in enumerate(out_refs):
        out_ref[...] = in_ref[pl.ds(pl.multiple_of((place_ref[0] + d) % 4 * 400, 16), 400), :]


def total_kernel(a_ref, b_ref, c_ref, d_ref, out_ref, total, split):
    parts = [ref[...].astype(F32) for ref in (a_ref, b_ref, c_ref, d_ref)]
    total[...] = (parts[0] + parts[1]) + (parts[2] + parts[3])
    for j in range(JD):
        v = total[pl.ds(j, SP, stride=JD), :]
        split[pl.ds(j * S, SP, stride=2), :] = v
        split[pl.ds(j * S + 1, SP, stride=2), :] = roll(v, 64)
    for j in range(JD):
        out_ref[j] = split[j * S : (j + 1) * S, 0:64]


def pack_kernel(in_ref, out_ref, rows, packed):
    for j in range(JD):
        rows[j * S : (j + 1) * S, 0:64] = in_ref[j].astype(F32)
    low = lanes(JD) < 64
    for p in range(SP):
        even, odd = rows[pl.ds(2 * p, JD, stride=S), :], rows[pl.ds(2 * p + 1, JD, stride=S), :]
        packed[p * JD : (p + 1) * JD, :] = jnp.where(low, even, roll(odd, 64))
    out_ref[...] = packed[...].astype(BF16)


def legendre_back_kernel(seeds_hbm, masked_hbm, out_ref, got, turn, waves, out, seeds, masked, come, come2):
    copies = [
        pltpu.make_async_copy(seeds_hbm.at[pl.ds(n * 1600, 1600)], seeds.at[pl.ds(n * 1600, 1600)], come.at[n])
        for n in range(8)
    ]
    later = [
        pltpu.make_async_copy(masked_hbm.at[pl.ds(2 * g, 2)], masked.at[pl.ds(2 * g, 2)], come2.at[g])
        for g in range(S // 4)
    ]
    for copy in copies + later:
        copy.start()
    turn[...] = jnp.zeros_like(turn)
    for n in range(8):
        copies[n].wait()
        rows = pl.ds(n * 1600, 1600)
        got[rows, :] = seeds[rows, :].astype(F32)
    lane = lanes(L)
    for g in range(S // 4):
        later[g].wait()
        starts = [n * 400 + g * 40 for n in range(32)]
        even = jnp.concatenate([got[at : at + 24, :] for at in starts], axis=0).astype(BF16)
        odd = jnp.concatenate([got[at + 16 : at + 40, :] for at in starts], axis=0).astype(BF16)
        right = jnp.concatenate([even, odd], axis=1)
        left = jnp.concatenate([masked[2 * g], masked[2 * g + 1]], axis=0)
        result = dot(left, right, 1, 0)
        for t in range(2):
            both = result[80 * t : 80 * t + 80, 128 * t : 128 * t + 128]
            turn[g % 2 * 2 + t, 0:L, :] = jnp.where(lane < 64, both[0:L], both[L : 2 * L])
            waves[(2 * g + t) * 128 : (2 * g + t + 1) * 128, :] = turn[g % 2 * 2 + t].T
    lane = lanes(Z)

    def rows_of(q, c2):
        i, r, b = q // (2 * BB), q // BB % 2, q % BB
        return waves[pl.ds((b * 8 + i) * 64 + r * 32 + c2 * Z, Z), :]

    for row in range(WR):
        first, second, third = row_pieces(row)
        v = rows_of(*first)
        v = jnp.where(lane >= 40, roll(rows_of(*second), 40), v)
        if third is not None:
            v = jnp.where(lane >= 80, roll(rows_of(*third), 80), v)
        out[pl.ds(row, Z, stride=WR), :] = v
    for d in range(Z):
        out_ref[d] = out[d * WR : (d + 1) * WR, :].astype(BF16)


def fourier_back_kernel(in_ref, table_ref, out_ref, got, waves, rests, out):
    for d in range(Z):
        got[d * WR : (d + 1) * WR, :] = in_ref[d].astype(F32)
    lane = lanes(Z)

    def piece(q, c2):
        row, place = wave_piece(q, c2)
        return roll(got[pl.ds(row, Z, stride=WR), :], 40 * (c2 - place))

    for i in range(8):
        p, m = (i % 4, i // 4) if i % 4 == 0 else (min(i, 8 - i), int(i > 4))
        for r in range(2):
            for b in range(BB):
                q = (i * 2 + r) * BB + b
                v = jnp.where(lane < 40, piece(q, 0), piece(q, 1))
                v = jnp.where(lane < 80, v, 0.0)
                at = p * 384 + (m * 2 + r) * NB + b * Z
                waves[at : at + Z, :] = v
    pairs = []
    for p in range(4):
        waves[p * 384 + 320 : p * 384 + 384, :] = jnp.zeros((64, 128), F32)
        left = jnp.concatenate(
            [waves[p * 384 + 128 * t : p * 384 + 128 * t + 128, :].T for t in range(3)], axis=1
        )
        left = left[0:80, 0:320].astype(BF16)
        pairs.append(dot(left, table_ref[p], 1, 0))
    for h in range(2):
        mains = [(v[:, 128 * h : 128 * h + 128], v[:, 256 + 128 * h : 384 + 128 * h]) for v in pairs]
        for p, v in enumerate(eight_back(mains)):
            out[(2 * p + h) * GR : (2 * p + h) * GR + 80, :] = v
    lane = lanes(20)
    for p in range(4):
        rests[p * 80 : p * 80 + 80, :] = pairs[p][:, 512:640]
    for h in range(2):
        packed = []
        for p in range(4):
            halves = []
            for part in range(2):
                pos = part * 2 + h
                v = None
                for e in range(4):
                    at = p * 80 + 10 * e
                    rows = jnp.concatenate([rests[at : at + 10, :], rests[at + 40 : at + 50, :]], axis=0)
                    rows = roll(rows, 32 * (e - pos))
                    v = rows if v is None else jnp.where(lane >= 32 * e, rows, v)
                halves.append(v)
            packed.append(tuple(halves))
        for p, v in enumerate(eight_back(packed)):
            out[(2 * p + h) * GR + 80 : (2 * p + h) * GR + 100, :] = v
    for d in range(Z):
        out_ref[d] = out[d * GR : (d + 1) * GR, :].astype(BF16)


def prep_basis(own, basis):
    return call(
        prep_basis_kernel,
        "prep_basis",
        (shape((SP, 2 * L, JW)), shape((SP, JW, 128))),
        [
            pltpu.VMEM((5, L * S, 128), F32),
            pltpu.VMEM((2, 5, 128, 128), F32),
            pltpu.VMEM((2, J, 128), F32),
            pltpu.VMEM((2, JW, 128), F32),
        ],
        smem=1,
    )(own, basis)


def prep_table(block_slot):
    slots = jnp.arange(NB, dtype=jnp.int32)
    holder = jnp.sum(jnp.where(block_slot[None, :] == slots[:, None], slots[None, :], 0), axis=1)
    holder = holder.astype(jnp.int32)
    lane = np.arange(128)
    k = np.concatenate((lane, 160 + lane, 160 * (lane % 64 // 32) + 128 + lane % 32)).astype(np.int32)
    order = holder.reshape(Z, BB).T.reshape(NB)
    phase = (order[:, None] * k[None, :]) % 320
    angle = phase.astype(F32) * (2.0 * math.pi / 320)
    fine = 2.0 * math.pi * np.arange(8)[:, None] * k[None, :] / NLON
    scale = 1.0 / math.sqrt(NLON)
    ci = jnp.asarray((np.cos(fine) * scale).astype(np.float32))
    si = jnp.asarray((np.sin(fine) * scale).astype(np.float32))
    table = call(
        prep_table_kernel, "prep_table", shape((4, 320, 640)), []
    )(jnp.cos(angle), jnp.sin(angle), ci, si)
    return holder, table


def column_step(fields, weight_in, weight_out_t):
    return call(
        column_kernel,
        "column",
        (shape((Z, GR, 128)), shape((C, L * K))),
        [pltpu.VMEM((C * L, 128), F32), pltpu.VMEM((C * L, 128), F32), pltpu.VMEM((Z * GR, 128), F32)],
    )(fields, weight_in, weight_out_t)


def column_back(keep, chunks, weight_in, weight_out_t):
    return call(
        column_back_kernel,
        "column_back",
        shape((C, L, K)),
        [
            pltpu.VMEM((C * L, 128), F32),
            pltpu.VMEM((C * L, 128), F32),
            pltpu.VMEM((Z * GR, 128), F32),
            pltpu.VMEM((C, 640), F32),
        ],
    )(keep, chunks, weight_in, weight_out_t)


def fourier(chunks, table):
    return call(
        fourier_kernel,
        "fourier",
        shape((Z, WR, 128)),
        [
            pltpu.VMEM((Z * GR, 128), F32),
            pltpu.VMEM((80, 128), F32),
            pltpu.VMEM((2 * M, 128), F32),
            pltpu.VMEM((Z * WR, 128), F32),
        ],
    )(chunks, table)


def fourier_back(chunks, table):
    return call(
        fourier_back_kernel,
        "fourier_back",
        shape((Z, GR, 128)),
        [
            pltpu.VMEM((Z * WR, 128), F32),
            pltpu.VMEM((4 * 384, 128), F32),
            pltpu.VMEM((320, 128), F32),
            pltpu.VMEM((Z * GR, 128), F32),
        ],
    )(chunks, table)


def legendre(core, chunks, turned):
    half = (J * SP // 2, 128)
    return call(
        legendre_kernel,
        "legendre",
        (shape(half), shape(half)),
        [
            pltpu.VMEM((Z * WR, 128), F32),
            pltpu.VMEM((S // 4, 256, 256), BF16),
            pltpu.VMEM((J * SP, 128), F32),
            pltpu.VMEM((SP, JW, 128), BF16),
            pltpu.VMEM(half, BF16),
            pltpu.VMEM(half, BF16),
            pltpu.SemaphoreType.DMA((S // 4,)),
            pltpu.SemaphoreType.DMA((8,)),
        ],
        smem=1,
        hbm=(2,),
        out_hbm=True,
    )(core, chunks, turned)


def pack(seeds):
    return call(pack_kernel, "pack", shape((JD * SP, 128)), [pltpu.VMEM((JD * S, 128), F32), pltpu.VMEM((JD * SP, 128), F32)])(
        seeds
    )


def core_sum(mine, other):
    return call(core_sum_kernel, "core_sum", shape((J * SP // 2, 128)), [])(mine, other)


def chip_parts(place, sums):
    return call(parts_kernel, "chip_parts", (shape((400, 128)),) * 4, [], smem=1)(place, sums)


def total(parts):
    return call(
        total_kernel,
        "total",
        shape((JD, S, 2 * C), F32),
        [pltpu.VMEM((JD * SP, 128), F32), pltpu.VMEM((JD * S, 128), F32)],
    )(*parts)


def legendre_back(seeds, masked):
    return call(
        legendre_back_kernel,
        "legendre_back",
        shape((Z, WR, 128)),
        [
            pltpu.VMEM((J * SP, 128), F32),
            pltpu.VMEM((4, 128, 128), F32),
            pltpu.VMEM((S * 64, 128), F32),
            pltpu.VMEM((Z * WR, 128), F32),
            pltpu.VMEM((J * SP, 128), BF16),
            pltpu.VMEM((SP, 2 * L, JW), BF16),
            pltpu.SemaphoreType.DMA((8,)),
            pltpu.SemaphoreType.DMA((S // 4,)),
        ],
        hbm=(0, 1),
    )(seeds, masked)


def exchange(values):
    return lax.all_to_all(values, "lon", split_axis=0, concat_axis=0, tiled=True)


def position(axis):
    return lax.axis_index(axis).astype(jnp.int32).reshape(1)


def swap(values):
    return lax.ppermute(values, "core", [(0, 1), (1, 0)])


def after(values, earlier):
    return lax.optimization_barrier((values, earlier))[0]


def along(parts, axis):
    return [parts[0]] + [
        lax.ppermute(parts[d], axis, [(i, (i + d) % 4) for i in range(4)]) for d in (2, 1, 3)
    ]


def local(grid_fields, weight_in, weight_out, legendre_basis, block_slot, spectrum_grad):
    weight_out_t = weight_out.T
    seeds = lax.all_gather(pack(spectrum_grad), ("y", "x", "core"), axis=0, tiled=True)
    chunks, keep = column_step(grid_fields, weight_in, weight_out_t)
    chunks, block_slot, legendre_basis = lax.optimization_barrier((chunks, block_slot, legendre_basis))
    chunks = exchange(chunks)
    holder, table = prep_table(block_slot)
    own = lax.dynamic_slice_in_dim(holder, lax.axis_index("lon") * BB, BB)
    masked, turned = prep_basis(own, legendre_basis)
    waves = exchange(fourier(chunks, table))
    mine, other = legendre(position("core"), waves, turned)
    back = legendre_back(seeds, after(masked, other))
    sums = core_sum(mine, after(swap(other), back))
    chunks = fourier_back(after(exchange(back), sums), table)
    sums = lax.psum_scatter(sums, "x", scatter_dimension=0, tiled=True)
    parts = along(chip_parts(position("y"), after(sums, chunks)), "y")
    fields_grad = column_back(keep, exchange(chunks), weight_in, weight_out_t)
    spectrum = total(after(parts, fields_grad))
    return (spectrum, fields_grad)


def solution(mesh):
    split = Mesh(mesh.devices.reshape(4, 4, 2, Z), ("y", "x", "core", "lon"))
    lat = ("y", "x", "core")
    in_specs = (P(None, lat, "lon"), P(), P(), P(lat, "lon", None), P(), P(lat, "lon", None))
    out_specs = (P(lat, "lon", None), P(None, lat, "lon"))
    return jax.shard_map(local, mesh=split, in_specs=in_specs, out_specs=out_specs, check_vma=False)
```

```python
import math

import jax
import jax.numpy as jnp
import numpy as np
from jax import lax
from jax.experimental import pallas as pl
from jax.experimental.pallas import tpu as pltpu
from jax.sharding import Mesh
from jax.sharding import PartitionSpec as P

NLON = 2560
M = 640
F32 = jnp.float32
BF16 = jnp.bfloat16

C = 32
H = 256
L = 40
K = 160
Z = 16
S = 40
J = 640
JD = 20
SP = S // 2
BB = 5
NB = 80
GR = 104
WR = 56
JW = 32 * 24
VMEM = 40 * 1024 * 1024
VMEM_ALL = 60 * 1024 * 1024


def dot(a, b, da, db):
    return lax.dot_general(a, b, (((da,), (db,)), ((), ())), preferred_element_type=F32)


def lanes(rows):
    return lax.broadcasted_iota(jnp.int32, (rows, 128), 1)


def grid_row(c2, t):
    return c2 * 40 + t if t < 40 else 80 + c2 * 10 + t - 40


def wave_piece(q, c2):
    i, r, b = q // (2 * BB), q // BB % 2, q % BB
    s = b * 8 + i
    return s // 6 * 8 + s % 2 * 4 + r * 2 + c2, s // 2 % 3


def row_pieces(row):
    slots = [row // 8 * 6 + 2 * k + row // 4 % 2 for k in range(3)]
    return [(s % 8 * 2 + row // 2 % 2) * BB + s // 8 for s in slots if s < S], row % 2


def roll(v, shift):
    shift = shift % 128
    return v if shift == 0 else pltpu.roll(v, shift, 1)


def call(kernel, name, out_shape, scratch, smem=0, hbm=(), out_hbm=False, vmem=VMEM):
    def run(*args):
        specs = [
            pl.BlockSpec(memory_space=pltpu.SMEM if i < smem else pl.ANY if i in hbm else pltpu.VMEM)
            for i in range(len(args))
        ]
        one = not isinstance(out_shape, (tuple, list))
        outs = pl.BlockSpec(memory_space=pl.ANY if out_hbm else pltpu.VMEM)
        return pl.pallas_call(
            kernel,
            name=name,
            out_shape=out_shape,
            in_specs=specs,
            out_specs=outs if one else tuple(outs for _ in out_shape),
            scratch_shapes=scratch,
            compiler_params=pltpu.CompilerParams(vmem_limit_bytes=vmem),
            cost_estimate=pl.CostEstimate(flops=1_000_000, bytes_accessed=100_000, transcendentals=0),
        )(*args)

    return run


def fetch(source, target, sem):
    copy = pltpu.make_async_copy(source, target, sem)
    copy.start()
    copy.wait()


def fetched(*dims):
    return [pltpu.VMEM(dims, BF16), pltpu.SemaphoreType.DMA]


def shape(dims, dtype=BF16):
    return jax.ShapeDtypeStruct(dims, dtype)


def prep_basis_kernel(own_ref, basis_ref, masked_ref, turned_ref, bs, tmp, column, wide):
    for row in range(L):
        v = basis_ref[row].astype(F32)
        for t in range(5):
            bs[t, row * S : (row + 1) * S, :] = v[:, 128 * t : 128 * t + 128]
    tmp[...] = jnp.zeros_like(tmp)
    wide[...] = jnp.zeros_like(wide)
    lane = lanes(L)

    def two_pairs(g, carry):
        for odd in range(2):
            p = 2 * g + odd
            for t in range(5):
                for e in range(2):
                    s = 2 * p + e
                    wave = own_ref[s // 8] * 8 + s % 8
                    v = bs[t, pl.ds(s, L, stride=S), :]
                    tmp[odd, t, 64 * e : 64 * e + L, :] = jnp.where(lane + 128 * t + wave <= M - 1, v, 0.0)
                column[odd, 128 * t : 128 * t + 128, :] = tmp[odd, t].T
            for n in range(32):
                at = 24 * n + 4 * odd
                wide[odd, at : at + JD, :] = column[odd, JD * n : JD * n + JD, :]
            turned_ref[p] = wide[odd].astype(BF16)
            for t in range(6):
                v = wide[odd, 128 * t : 128 * t + 128, :].T
                both = jnp.concatenate([v[0:L], v[64 : 64 + L]], axis=0).astype(BF16)
                masked_ref[p, :, 128 * t : 128 * t + 128] = both
        return carry

    lax.fori_loop(0, SP // 2, two_pairs, 0)


def prep_table_kernel(cb_ref, sb_ref, ci_ref, si_ref, table_ref):
    low = lanes(NB) < 64

    def angle(i, t):
        cb, sb = cb_ref[:, 128 * t : 128 * t + 128], sb_ref[:, 128 * t : 128 * t + 128]
        ci, si = ci_ref[i : i + 1, 128 * t : 128 * t + 128], si_ref[i : i + 1, 128 * t : 128 * t + 128]
        return cb * ci - sb * si, sb * ci + cb * si

    for p in range(4):
        for m, i in enumerate((p, 8 - p) if p else (0, 4)):
            for t in range(3):
                c, s = angle(i, t)
                zero = jnp.zeros_like(c)
                if p == 0:
                    first, second = (c, -s), (zero, zero)
                    if m == 1:
                        first, second = second, first
                elif m == 0:
                    first, second = (c, -s), (s, c)
                else:
                    first, second = (c, -s), (-s, -c)
                for r in range(2):
                    rows = slice((m * 2 + r) * NB, (m * 2 + r + 1) * NB)
                    if t < 2:
                        table_ref[p, rows, 128 * t : 128 * t + 128] = first[r].astype(BF16)
                        table_ref[p, rows, 256 + 128 * t : 384 + 128 * t] = second[r].astype(BF16)
                    else:
                        both = jnp.where(low, first[r], second[r])
                        table_ref[p, rows, 512:640] = both.astype(BF16)


def column_kernel(x_ref, win_ref, wout_ref, seeds_ref, out_ref, keep_ref, pack_ref, main, rest, out, rows, packed):
    for j in range(JD):
        rows[j * S : (j + 1) * S, 0:64] = seeds_ref[j].astype(F32)
    low = lanes(JD) < 64
    for p in range(SP):
        even, odd = rows[pl.ds(2 * p, JD, stride=S), :], rows[pl.ds(2 * p + 1, JD, stride=S), :]
        packed[p * JD : (p + 1) * JD, :] = jnp.where(low, even, roll(odd, 64))
    pack_ref[...] = packed[...].astype(BF16)
    for c in range(C):
        v = x_ref[c].astype(F32)
        main[c * L : (c + 1) * L, :] = v[:, :128]
        rest[c * L : (c + 1) * L, 0:32] = v[:, 128:K]
    lane = lanes(C)
    for t in range(50):
        if t < 40:
            v = main[pl.ds(t, C, stride=L), :]
        else:
            v = rest[pl.ds(t - 40, C, stride=L), :]
            for e in range(1, 4):
                v = jnp.where(lane >= 32 * e, roll(rest[pl.ds(t - 40 + 10 * e, C, stride=L), :], 32 * e), v)
        keep_ref[:, 128 * t : 128 * t + 128] = v.astype(BF16)
    win, wout = win_ref[...], wout_ref[...]
    for chunk in range(10):
        x = keep_ref[:, 640 * chunk : 640 * chunk + 640]
        pre = dot(win, x, 0, 0)
        half = 0.5 * pre
        active = (half + half * jnp.tanh(half)).astype(BF16)
        y = x.astype(F32) + dot(wout, active, 1, 0)
        for k in range(5):
            for c2 in range(2):
                row = grid_row(c2, 5 * chunk + k)
                out[pl.ds(row, Z, stride=GR), :] = y[Z * c2 : Z * c2 + Z, 128 * k : 128 * k + 128]
    for d in range(Z):
        out_ref[d] = out[d * GR : (d + 1) * GR, :].astype(BF16)


def slope_kernel(keep_ref, win_ref, out_ref):
    win = win_ref[...]
    for chunk in range(10):
        part = slice(640 * chunk, 640 * chunk + 640)
        pre = dot(win, keep_ref[:, part], 0, 0)
        sigma = 0.5 + 0.5 * jnp.tanh(0.5 * pre)
        out_ref[:, part] = (sigma * (1.0 + pre * (1.0 - sigma))).astype(BF16)


def column_back_kernel(slope_hbm, g_hbm, win_ref, wout_ref, out_ref, main, rest, got, up, slope, come, g_ref, sem):
    copies = []
    for chunk in range(10):
        part = pl.ds(640 * chunk, 640)
        copies.append(pltpu.make_async_copy(slope_hbm.at[:, part], slope.at[:, part], come.at[chunk]))
        copies[-1].start()
    fetch(g_hbm, g_ref, sem)
    for d in range(Z):
        got[d * GR : (d + 1) * GR, :] = g_ref[d].astype(F32)
    win, wout = win_ref[...], wout_ref[...]
    for chunk in range(10):
        for k in range(5):
            t = 5 * chunk + k
            for c2 in range(2):
                up[Z * c2 : Z * c2 + Z, 128 * k : 128 * k + 128] = got[pl.ds(grid_row(c2, t), Z, stride=GR), :]
        upstream = up[...]
        act_grad = dot(wout, upstream.astype(BF16), 0, 0)
        copies[chunk].wait()
        pre_grad = (act_grad * slope[:, 640 * chunk : 640 * chunk + 640].astype(F32)).astype(BF16)
        y = upstream + dot(win, pre_grad, 1, 0)
        for k in range(5):
            t = 5 * chunk + k
            v = y[:, 128 * k : 128 * k + 128]
            if t < 40:
                main[pl.ds(t, C, stride=L), :] = v
            else:
                for e in range(4):
                    rest[pl.ds(t - 40 + 10 * e, C, stride=L), :] = roll(v, -32 * e)
    for c in range(C):
        out_ref[c, :, 0:128] = main[c * L : (c + 1) * L, :].astype(BF16)
        out_ref[c, :, 128:K] = rest[c * L : (c + 1) * L, 0:32].astype(BF16)


def eight(x):
    root = math.sqrt(0.5)
    s = [x[p] + x[p + 4] for p in range(4)]
    d = [x[p] - x[p + 4] for p in range(4)]
    e0, e1, o0, o1 = s[0] + s[2], s[0] - s[2], s[1] + s[3], s[1] - s[3]
    u, v = root * (d[1] - d[3]), root * (d[1] + d[3])
    return [(e0 + o0, e0 - o0), (d[0] + u, -d[2] - v), (e1, -o1), (d[0] - u, d[2] - v)]


def eight_back(pairs):
    root = math.sqrt(0.5)
    (a0, b0), (a1, b1), (a2, b2), (a3, b3) = pairs
    plus, minus = a0 + b0, a0 - b0
    sa, da, sb, db = a1 + a3, a1 - a3, b1 + b3, b1 - b3
    even0, even2 = plus + a2, plus - a2
    odd1, odd3 = minus - b2, minus + b2
    u, v = root * da, root * sb
    return [
        even0 + sa,
        odd1 + (u - v),
        even2 - db,
        odd3 - (u + v),
        even0 - sa,
        odd1 - (u - v),
        even2 + db,
        odd3 + (u + v),
    ]


def fourier_kernel(in_hbm, table_ref, out_ref, got, low, waves, out, in_ref, sem):
    fetch(in_hbm, in_ref, sem)
    for d in range(Z):
        got[d * GR : (d + 1) * GR, :] = in_ref[d].astype(F32)
    lane = lanes(20)
    mains = [[], []]
    packed = [[], []]
    for h in range(2):
        mains[h] = eight([got[(2 * p + h) * GR : (2 * p + h) * GR + 80, :] for p in range(8)])
        packed[h] = eight([got[(2 * p + h) * GR + 80 : (2 * p + h) * GR + 100, :] for p in range(8)])
    for i in range(4):
        parts = [packed[pos % 2][i][pos // 2] for pos in range(4)]
        for e in range(4):
            v = roll(parts[0], -32 * e)
            for pos in range(1, 4):
                v = jnp.where(lane >= 32 * pos, roll(parts[pos], 32 * (pos - e)), v)
            low[10 * e : 10 * e + 10, :] = v[0:10]
            low[40 + 10 * e : 50 + 10 * e, :] = v[10:20]
        left = jnp.concatenate(
            [mains[0][i][0], mains[1][i][0], mains[0][i][1], mains[1][i][1], low[0:80, :]], axis=1
        ).astype(BF16)
        left = jnp.concatenate([left, jnp.zeros((48, 640), BF16)], axis=0)
        result = dot(table_ref[i], left, 1, 1)
        for m, w in enumerate((i, 8 - i) if i else (0, 4)):
            waves[w * 160 : w * 160 + 160, :] = result[m * 160 : m * 160 + 160]
    lane = lanes(Z)
    for row in range(WR):
        parts, c2 = row_pieces(row)
        v = None
        for k, q in enumerate(parts):
            piece = roll(waves[q * Z : q * Z + Z, :], 40 * (k - c2))
            v = piece if v is None else jnp.where(lane >= 40 * k, piece, v)
        out[pl.ds(row, Z, stride=WR), :] = v
    for d in range(Z):
        out_ref[d] = out[d * WR : (d + 1) * WR, :].astype(BF16)


def legendre_kernel(in_hbm, turned_hbm, out_hbm, got, three, block, turned, out, come, go, in_ref, sem):
    copies = [
        pltpu.make_async_copy(turned_hbm.at[pl.ds(4 * n, 4)], turned.at[pl.ds(4 * n, 4)], come.at[n])
        for n in range(5)
    ]
    for copy in copies:
        copy.start()
    fetch(in_hbm, in_ref, sem)
    for d in range(Z):
        got[d * WR : (d + 1) * WR, :] = in_ref[d].astype(F32)
    zero = jnp.zeros((128, 128), BF16)
    gap = jnp.zeros((24, 128), F32)
    low = lanes(L) < 64
    for p3 in range(7):
        for row in range(8):
            three[p3, row * Z : row * Z + Z, :] = got[pl.ds(p3 * 8 + row, Z, stride=WR), :]
        v3 = three[p3].T
        for p in range(3 * p3, min(3 * p3 + 3, SP)):
            v = v3[(p % 3) * L : (p % 3) * L + L]
            both = jnp.concatenate([jnp.where(low, v, 0.0), gap, jnp.where(low, 0.0, v), gap], axis=0)
            here, there = 128 * (p % 2), 128 - 128 * (p % 2)
            block[p // 2, here : here + 128, here : here + 128] = both.astype(BF16)
            block[p // 2, here : here + 128, there : there + 128] = zero
    stores = []
    for step in range(5):
        copies[step].wait()
        results = []
        for g in (2 * step, 2 * step + 1):
            left = jnp.concatenate([turned[2 * g], turned[2 * g + 1]], axis=1)
            results.append(dot(left, block[g], 1, 0))
        for n in range(32):
            rows = []
            for result in results:
                even, odd = result[24 * n : 24 * n + 24, 0:128], result[24 * n : 24 * n + 24, 128:256]
                rows += [even[0:16], even[16:24] + odd[0:8], odd[8:24]]
            place = n % 8 * 4 + n // 8
            out[place, 80 * step : 80 * step + 80, :] = jnp.concatenate(rows, axis=0).astype(BF16)
        part = pl.ds(80 * step, 80)
        stores.append(pltpu.make_async_copy(out.at[:, part], out_hbm.at[:, part], go.at[step]))
        stores[-1].start()
    for copy in stores:
        copy.wait()


def parts_kernel(place_ref, in_ref, *out_refs):
    for d, out_ref in enumerate(out_refs):
        out_ref[...] = in_ref[pl.ds(pl.multiple_of((place_ref[0] + d) % 4 * 400, 16), 400), :]


def total_kernel(a_ref, b_ref, c_ref, d_ref, out_ref, total, split):
    parts = [ref[...].astype(F32) for ref in (a_ref, b_ref, c_ref, d_ref)]
    total[...] = (parts[0] + parts[1]) + (parts[2] + parts[3])
    for j in range(JD):
        v = total[pl.ds(j, SP, stride=JD), :]
        split[pl.ds(j * S, SP, stride=2), :] = v
        split[pl.ds(j * S + 1, SP, stride=2), :] = roll(v, 64)
    for j in range(JD):
        out_ref[j] = split[j * S : (j + 1) * S, 0:64]


def legendre_back_kernel(seeds_hbm, masked_hbm, out_ref, three, out, seeds, masked, come, come2):
    copies, later = [], []
    for step in range(5):
        part, pairs = pl.ds(80 * step, 80), pl.ds(4 * step, 4)
        copies.append(pltpu.make_async_copy(seeds_hbm.at[:, part], seeds.at[:, part], come.at[step]))
        later.append(pltpu.make_async_copy(masked_hbm.at[pairs], masked.at[pairs], come2.at[step]))
        copies[-1].start()
        later[-1].start()
    three[...] = jnp.zeros_like(three)
    low = lanes(L) < 64
    for step in range(5):
        copies[step].wait()
        later[step].wait()
        values = [seeds[n, 80 * step : 80 * step + 80, :].astype(F32) for n in range(32)]
        for g in (2 * step, 2 * step + 1):
            at = g % 2 * 40
            even = jnp.concatenate([v[at : at + 24] for v in values], axis=0).astype(BF16)
            odd = jnp.concatenate([v[at + 16 : at + 40] for v in values], axis=0).astype(BF16)
            right = jnp.concatenate([even, odd], axis=1)
            left = jnp.concatenate([masked[2 * g], masked[2 * g + 1]], axis=0)
            result = dot(left, right, 1, 0)
            for t in range(2):
                p = 2 * g + t
                both = result[80 * t : 80 * t + 80, 128 * t : 128 * t + 128]
                three[p // 3, p % 3 * L : p % 3 * L + L, :] = jnp.where(low, both[0:L], both[L : 2 * L])
    for p3 in range(7):
        v = three[p3].T
        for row in range(8):
            out[pl.ds(p3 * 8 + row, Z, stride=WR), :] = v[row * Z : row * Z + Z]
    for d in range(Z):
        out_ref[d] = out[d * WR : (d + 1) * WR, :].astype(BF16)


def fourier_back_kernel(in_hbm, table_ref, out_ref, got, waves, rests, out, in_ref, sem):
    fetch(in_hbm, in_ref, sem)
    for d in range(Z):
        got[d * WR : (d + 1) * WR, :] = in_ref[d].astype(F32)
    lane = lanes(Z)

    def piece(q, c2):
        row, place = wave_piece(q, c2)
        return roll(got[pl.ds(row, Z, stride=WR), :], 40 * (c2 - place))

    for i in range(8):
        p, m = (i % 4, i // 4) if i % 4 == 0 else (min(i, 8 - i), int(i > 4))
        for r in range(2):
            for b in range(BB):
                q = (i * 2 + r) * BB + b
                v = jnp.where(lane < 40, piece(q, 0), piece(q, 1))
                v = jnp.where(lane < 80, v, 0.0)
                at = p * 384 + (m * 2 + r) * NB + b * Z
                waves[at : at + Z, :] = v
    pairs = []
    for p in range(4):
        waves[p * 384 + 320 : p * 384 + 384, :] = jnp.zeros((64, 128), F32)
        left = jnp.concatenate(
            [waves[p * 384 + 128 * t : p * 384 + 128 * t + 128, :].T for t in range(3)], axis=1
        )
        left = left[0:80, 0:320].astype(BF16)
        pairs.append(dot(left, table_ref[p], 1, 0))
    for h in range(2):
        mains = [(v[:, 128 * h : 128 * h + 128], v[:, 256 + 128 * h : 384 + 128 * h]) for v in pairs]
        for p, v in enumerate(eight_back(mains)):
            out[(2 * p + h) * GR : (2 * p + h) * GR + 80, :] = v
    lane = lanes(20)
    for p in range(4):
        rests[p * 80 : p * 80 + 80, :] = pairs[p][:, 512:640]
    for h in range(2):
        packed = []
        for p in range(4):
            halves = []
            for part in range(2):
                pos = part * 2 + h
                v = None
                for e in range(4):
                    at = p * 80 + 10 * e
                    rows = jnp.concatenate([rests[at : at + 10, :], rests[at + 40 : at + 50, :]], axis=0)
                    rows = roll(rows, 32 * (e - pos))
                    v = rows if v is None else jnp.where(lane >= 32 * e, rows, v)
                halves.append(v)
            packed.append(tuple(halves))
        for p, v in enumerate(eight_back(packed)):
            out[(2 * p + h) * GR + 80 : (2 * p + h) * GR + 100, :] = v
    for d in range(Z):
        out_ref[d] = out[d * GR : (d + 1) * GR, :].astype(BF16)


def prep_basis(own, basis):
    return call(
        prep_basis_kernel,
        "prep_basis",
        (shape((SP, 2 * L, JW)), shape((SP, JW, 128))),
        [
            pltpu.VMEM((5, L * S, 128), F32),
            pltpu.VMEM((2, 5, 128, 128), F32),
            pltpu.VMEM((2, J, 128), F32),
            pltpu.VMEM((2, JW, 128), F32),
        ],
        smem=1,
        vmem=VMEM_ALL,
    )(own, basis)


def prep_table(block_slot):
    slots = jnp.arange(NB, dtype=jnp.int32)
    holder = jnp.sum(jnp.where(block_slot[None, :] == slots[:, None], slots[None, :], 0), axis=1)
    holder = holder.astype(jnp.int32)
    lane = np.arange(128)
    k = np.concatenate((lane, 160 + lane, 160 * (lane % 64 // 32) + 128 + lane % 32)).astype(np.int32)
    order = holder.reshape(Z, BB).T.reshape(NB)
    phase = (order[:, None] * k[None, :]) % 320
    angle = phase.astype(F32) * (2.0 * math.pi / 320)
    fine = 2.0 * math.pi * np.arange(8)[:, None] * k[None, :] / NLON
    scale = 1.0 / math.sqrt(NLON)
    ci = jnp.asarray((np.cos(fine) * scale).astype(np.float32))
    si = jnp.asarray((np.sin(fine) * scale).astype(np.float32))
    table = call(
        prep_table_kernel, "prep_table", shape((4, 320, 640)), []
    )(jnp.cos(angle), jnp.sin(angle), ci, si)
    return holder, table


def column_step(fields, weight_in, weight_out_t, seeds):
    return call(
        column_kernel,
        "column",
        (shape((Z, GR, 128)), shape((C, L * K)), shape((JD * SP, 128))),
        [
            pltpu.VMEM((C * L, 128), F32),
            pltpu.VMEM((C * L, 128), F32),
            pltpu.VMEM((Z * GR, 128), F32),
            pltpu.VMEM((JD * S, 128), F32),
            pltpu.VMEM((JD * SP, 128), F32),
        ],
        vmem=VMEM_ALL,
    )(fields, weight_in, weight_out_t, seeds)


def slope(keep, weight_in):
    return call(slope_kernel, "slope", shape((H, L * K)), [])(keep, weight_in)


def column_back(slopes, chunks, weight_in, weight_out_t):
    return call(
        column_back_kernel,
        "column_back",
        shape((C, L, K)),
        [
            pltpu.VMEM((C * L, 128), F32),
            pltpu.VMEM((C * L, 128), F32),
            pltpu.VMEM((Z * GR, 128), F32),
            pltpu.VMEM((C, 640), F32),
            pltpu.VMEM((H, L * K), BF16),
            pltpu.SemaphoreType.DMA((10,)),
            *fetched(Z, GR, 128),
        ],
        hbm=(0, 1),
    )(slopes, chunks, weight_in, weight_out_t)


def fourier(chunks, table):
    return call(
        fourier_kernel,
        "fourier",
        shape((Z, WR, 128)),
        [
            pltpu.VMEM((Z * GR, 128), F32),
            pltpu.VMEM((80, 128), F32),
            pltpu.VMEM((2 * M, 128), F32),
            pltpu.VMEM((Z * WR, 128), F32),
            *fetched(Z, GR, 128),
        ],
        hbm=(0,),
    )(chunks, table)


def fourier_back(chunks, table):
    return call(
        fourier_back_kernel,
        "fourier_back",
        shape((Z, GR, 128)),
        [
            pltpu.VMEM((Z * WR, 128), F32),
            pltpu.VMEM((4 * 384, 128), F32),
            pltpu.VMEM((320, 128), F32),
            pltpu.VMEM((Z * GR, 128), F32),
            *fetched(Z, WR, 128),
        ],
        hbm=(0,),
    )(chunks, table)


def legendre(chunks, turned):
    return call(
        legendre_kernel,
        "legendre",
        shape((32, JD * SP, 128)),
        [
            pltpu.VMEM((Z * WR, 128), F32),
            pltpu.VMEM((7, 128, 128), F32),
            pltpu.VMEM((S // 4, 256, 256), BF16),
            pltpu.VMEM((SP, JW, 128), BF16),
            pltpu.VMEM((32, JD * SP, 128), BF16),
            pltpu.SemaphoreType.DMA((5,)),
            pltpu.SemaphoreType.DMA((5,)),
            *fetched(Z, WR, 128),
        ],
        hbm=(0, 1),
        out_hbm=True,
        vmem=VMEM_ALL,
    )(chunks, turned)


def chip_parts(place, sums):
    return call(parts_kernel, "chip_parts", (shape((400, 128)),) * 4, [], smem=1)(place, sums)


def total(parts):
    return call(
        total_kernel,
        "total",
        shape((JD, S, 2 * C), F32),
        [pltpu.VMEM((JD * SP, 128), F32), pltpu.VMEM((JD * S, 128), F32)],
    )(*parts)


def legendre_back(seeds, masked):
    return call(
        legendre_back_kernel,
        "legendre_back",
        shape((Z, WR, 128)),
        [
            pltpu.VMEM((7, 128, 128), F32),
            pltpu.VMEM((Z * WR, 128), F32),
            pltpu.VMEM((32, JD * SP, 128), BF16),
            pltpu.VMEM((SP, 2 * L, JW), BF16),
            pltpu.SemaphoreType.DMA((5,)),
            pltpu.SemaphoreType.DMA((5,)),
        ],
        hbm=(0, 1),
        vmem=VMEM_ALL,
    )(seeds.reshape(32, JD * SP, 128), masked)


def exchange(values):
    return lax.all_to_all(values, "lon", split_axis=0, concat_axis=0, tiled=True)


def position(axis):
    return lax.axis_index(axis).astype(jnp.int32).reshape(1)


def after(values, earlier):
    return lax.optimization_barrier((values, earlier))[0]


def along(parts, axis):
    return [parts[0]] + [
        lax.ppermute(parts[d], axis, [(i, (i + d) % 4) for i in range(4)]) for d in (2, 1, 3)
    ]


def local(grid_fields, weight_in, weight_out, legendre_basis, block_slot, spectrum_grad):
    weight_out_t = weight_out.T
    chunks, keep, seeds = column_step(grid_fields, weight_in, weight_out_t, spectrum_grad)
    seeds = lax.all_gather(seeds, ("y", "x", "core"), axis=0, tiled=True)
    chunks, block_slot, legendre_basis = lax.optimization_barrier((chunks, block_slot, legendre_basis))
    chunks = exchange(chunks)
    holder, table = prep_table(block_slot)
    own = lax.dynamic_slice_in_dim(holder, lax.axis_index("lon") * BB, BB)
    masked, turned = prep_basis(own, legendre_basis)
    waves = exchange(fourier(chunks, table))
    sums = legendre(waves, turned)
    back = legendre_back(seeds, after(masked, sums))
    sums = lax.psum_scatter(sums.reshape(J * SP, 128), ("x", "core"), scatter_dimension=0, tiled=True)
    chunks = fourier_back(exchange(back), table)
    slopes = slope(after(keep, chunks), weight_in)
    parts = along(chip_parts(position("y"), after(sums, slopes)), "y")
    fields_grad = column_back(slopes, exchange(chunks), weight_in, weight_out_t)
    spectrum = total(after(parts, fields_grad))
    return (spectrum, fields_grad)


def solution(mesh):
    split = Mesh(mesh.devices.reshape(4, 4, 2, Z), ("y", "x", "core", "lon"))
    lat = ("y", "x", "core")
    in_specs = (P(None, lat, "lon"), P(), P(), P(lat, "lon", None), P(), P(lat, "lon", None))
    out_specs = (P(lat, "lon", None), P(None, lat, "lon"))
    return jax.shard_map(local, mesh=split, in_specs=in_specs, out_specs=out_specs, check_vma=False)
```

```python
import math

import jax
import jax.numpy as jnp
import numpy as np
from jax import lax
from jax.experimental import pallas as pl
from jax.experimental.pallas import tpu as pltpu
from jax.sharding import Mesh
from jax.sharding import PartitionSpec as P

NLON = 2560
M = 640
F32 = jnp.float32
BF16 = jnp.bfloat16

C = 32
H = 256
L = 40
K = 160
Z = 16
S = 40
J = 640
JD = 20
SP = S // 2
BB = 5
NB = 80
GR = 104
WR = 56
JW = 32 * 24
VMEM = 40 * 1024 * 1024
VMEM_ALL = 60 * 1024 * 1024


def dot(a, b, da, db):
    return lax.dot_general(a, b, (((da,), (db,)), ((), ())), preferred_element_type=F32)


def lanes(rows):
    return lax.broadcasted_iota(jnp.int32, (rows, 128), 1)


def grid_row(c2, t):
    return c2 * 40 + t if t < 40 else 80 + c2 * 10 + t - 40


def wave_piece(q, c2):
    i, r, b = q // (2 * BB), q // BB % 2, q % BB
    s = b * 8 + i
    return s // 6 * 8 + s % 2 * 4 + r * 2 + c2, s // 2 % 3


def row_pieces(row):
    slots = [row // 8 * 6 + 2 * k + row // 4 % 2 for k in range(3)]
    return [(s % 8 * 2 + row // 2 % 2) * BB + s // 8 for s in slots if s < S], row % 2


def roll(v, shift):
    shift = shift % 128
    return v if shift == 0 else pltpu.roll(v, shift, 1)


def call(kernel, name, out_shape, scratch, smem=0, hbm=(), out_hbm=False, vmem=VMEM):
    def run(*args):
        specs = [
            pl.BlockSpec(memory_space=pltpu.SMEM if i < smem else pl.ANY if i in hbm else pltpu.VMEM)
            for i in range(len(args))
        ]
        one = not isinstance(out_shape, (tuple, list))
        outs = pl.BlockSpec(memory_space=pl.ANY if out_hbm else pltpu.VMEM)
        return pl.pallas_call(
            kernel,
            name=name,
            out_shape=out_shape,
            in_specs=specs,
            out_specs=outs if one else tuple(outs for _ in out_shape),
            scratch_shapes=scratch,
            compiler_params=pltpu.CompilerParams(vmem_limit_bytes=vmem),
            cost_estimate=pl.CostEstimate(flops=1_000_000, bytes_accessed=100_000, transcendentals=0),
        )(*args)

    return run


def fetch(source, target, sem):
    copy = pltpu.make_async_copy(source, target, sem)
    copy.start()
    copy.wait()


def fetched(*dims):
    return [pltpu.VMEM(dims, BF16), pltpu.SemaphoreType.DMA]


def shape(dims, dtype=BF16):
    return jax.ShapeDtypeStruct(dims, dtype)


def prep_basis_kernel(own_ref, basis_ref, masked_ref, turned_ref, bs, tmp, column, wide):
    for row in range(L):
        v = basis_ref[row].astype(F32)
        for t in range(5):
            bs[t, row * S : (row + 1) * S, :] = v[:, 128 * t : 128 * t + 128]
    tmp[...] = jnp.zeros_like(tmp)
    wide[...] = jnp.zeros_like(wide)
    lane = lanes(L)

    def two_pairs(g, carry):
        for odd in range(2):
            p = 2 * g + odd
            for t in range(5):
                for e in range(2):
                    s = 2 * p + e
                    wave = own_ref[s // 8] * 8 + s % 8
                    v = bs[t, pl.ds(s, L, stride=S), :]
                    tmp[odd, t, 64 * e : 64 * e + L, :] = jnp.where(lane + 128 * t + wave <= M - 1, v, 0.0)
                column[odd, 128 * t : 128 * t + 128, :] = tmp[odd, t].T
            for n in range(32):
                at = 24 * n + 4 * odd
                wide[odd, at : at + JD, :] = column[odd, JD * n : JD * n + JD, :]
            turned_ref[p] = wide[odd].astype(BF16)
            for t in range(6):
                v = wide[odd, 128 * t : 128 * t + 128, :].T
                both = jnp.concatenate([v[0:L], v[64 : 64 + L]], axis=0).astype(BF16)
                masked_ref[p, :, 128 * t : 128 * t + 128] = both
        return carry

    lax.fori_loop(0, SP // 2, two_pairs, 0)


def prep_table_kernel(cb_ref, sb_ref, ci_ref, si_ref, table_ref):
    low = lanes(NB) < 64

    def angle(i, t):
        cb, sb = cb_ref[:, 128 * t : 128 * t + 128], sb_ref[:, 128 * t : 128 * t + 128]
        ci, si = ci_ref[i : i + 1, 128 * t : 128 * t + 128], si_ref[i : i + 1, 128 * t : 128 * t + 128]
        return cb * ci - sb * si, sb * ci + cb * si

    for p in range(4):
        for m, i in enumerate((p, 8 - p) if p else (0, 4)):
            for t in range(3):
                c, s = angle(i, t)
                zero = jnp.zeros_like(c)
                if p == 0:
                    first, second = (c, -s), (zero, zero)
                    if m == 1:
                        first, second = second, first
                elif m == 0:
                    first, second = (c, -s), (s, c)
                else:
                    first, second = (c, -s), (-s, -c)
                for r in range(2):
                    rows = slice((m * 2 + r) * NB, (m * 2 + r + 1) * NB)
                    if t < 2:
                        table_ref[p, rows, 128 * t : 128 * t + 128] = first[r].astype(BF16)
                        table_ref[p, rows, 256 + 128 * t : 384 + 128 * t] = second[r].astype(BF16)
                    else:
                        both = jnp.where(low, first[r], second[r])
                        table_ref[p, rows, 512:640] = both.astype(BF16)


def column_kernel(x_ref, win_ref, wout_ref, seeds_ref, out_ref, keep_ref, pack_ref, main, rest, out, rows, packed):
    for j in range(JD):
        rows[j * S : (j + 1) * S, 0:64] = seeds_ref[j].astype(F32)
    low = lanes(JD) < 64
    for p in range(SP):
        even, odd = rows[pl.ds(2 * p, JD, stride=S), :], rows[pl.ds(2 * p + 1, JD, stride=S), :]
        packed[p * JD : (p + 1) * JD, :] = jnp.where(low, even, roll(odd, 64))
    pack_ref[...] = packed[...].astype(BF16)
    for c in range(C):
        v = x_ref[c].astype(F32)
        main[c * L : (c + 1) * L, :] = v[:, :128]
        rest[c * L : (c + 1) * L, 0:32] = v[:, 128:K]
    lane = lanes(C)
    for t in range(50):
        if t < 40:
            v = main[pl.ds(t, C, stride=L), :]
        else:
            v = rest[pl.ds(t - 40, C, stride=L), :]
            for e in range(1, 4):
                v = jnp.where(lane >= 32 * e, roll(rest[pl.ds(t - 40 + 10 * e, C, stride=L), :], 32 * e), v)
        keep_ref[:, 128 * t : 128 * t + 128] = v.astype(BF16)
    win, wout = win_ref[...], wout_ref[...]
    for chunk in range(10):
        x = keep_ref[:, 640 * chunk : 640 * chunk + 640]
        pre = dot(win, x, 0, 0)
        half = 0.5 * pre
        active = (half + half * jnp.tanh(half)).astype(BF16)
        y = x.astype(F32) + dot(wout, active, 1, 0)
        for k in range(5):
            for c2 in range(2):
                row = grid_row(c2, 5 * chunk + k)
                out[pl.ds(row, Z, stride=GR), :] = y[Z * c2 : Z * c2 + Z, 128 * k : 128 * k + 128]
    for d in range(Z):
        out_ref[d] = out[d * GR : (d + 1) * GR, :].astype(BF16)


def slope_kernel(keep_ref, win_ref, out_ref):
    win = win_ref[...]
    for chunk in range(10):
        part = slice(640 * chunk, 640 * chunk + 640)
        pre = dot(win, keep_ref[:, part], 0, 0)
        sigma = 0.5 + 0.5 * jnp.tanh(0.5 * pre)
        out_ref[:, part] = (sigma * (1.0 + pre * (1.0 - sigma))).astype(BF16)


def column_back_kernel(slope_hbm, g_hbm, win_ref, wout_ref, out_ref, main, rest, got, up, slope, come, g_ref, sem):
    first = pltpu.make_async_copy(g_hbm, g_ref, sem)
    first.start()
    copies = []
    for chunk in range(10):
        part = pl.ds(640 * chunk, 640)
        copies.append(pltpu.make_async_copy(slope_hbm.at[:, part], slope.at[:, part], come.at[chunk]))
        copies[-1].start()
    first.wait()
    for d in range(Z):
        got[d * GR : (d + 1) * GR, :] = g_ref[d].astype(F32)
    win, wout = win_ref[...], wout_ref[...]
    for chunk in range(10):
        for k in range(5):
            t = 5 * chunk + k
            for c2 in range(2):
                up[Z * c2 : Z * c2 + Z, 128 * k : 128 * k + 128] = got[pl.ds(grid_row(c2, t), Z, stride=GR), :]
        upstream = up[...]
        act_grad = dot(wout, upstream.astype(BF16), 0, 0)
        copies[chunk].wait()
        pre_grad = (act_grad * slope[:, 640 * chunk : 640 * chunk + 640].astype(F32)).astype(BF16)
        y = upstream + dot(win, pre_grad, 1, 0)
        for k in range(5):
            t = 5 * chunk + k
            v = y[:, 128 * k : 128 * k + 128]
            if t < 40:
                main[pl.ds(t, C, stride=L), :] = v
            else:
                for e in range(4):
                    rest[pl.ds(t - 40 + 10 * e, C, stride=L), :] = roll(v, -32 * e)
    for c in range(C):
        out_ref[c, :, 0:128] = main[c * L : (c + 1) * L, :].astype(BF16)
        out_ref[c, :, 128:K] = rest[c * L : (c + 1) * L, 0:32].astype(BF16)


def eight(x):
    root = math.sqrt(0.5)
    s = [x[p] + x[p + 4] for p in range(4)]
    d = [x[p] - x[p + 4] for p in range(4)]
    e0, e1, o0, o1 = s[0] + s[2], s[0] - s[2], s[1] + s[3], s[1] - s[3]
    u, v = root * (d[1] - d[3]), root * (d[1] + d[3])
    return [(e0 + o0, e0 - o0), (d[0] + u, -d[2] - v), (e1, -o1), (d[0] - u, d[2] - v)]


def eight_back(pairs):
    root = math.sqrt(0.5)
    (a0, b0), (a1, b1), (a2, b2), (a3, b3) = pairs
    plus, minus = a0 + b0, a0 - b0
    sa, da, sb, db = a1 + a3, a1 - a3, b1 + b3, b1 - b3
    even0, even2 = plus + a2, plus - a2
    odd1, odd3 = minus - b2, minus + b2
    u, v = root * da, root * sb
    return [
        even0 + sa,
        odd1 + (u - v),
        even2 - db,
        odd3 - (u + v),
        even0 - sa,
        odd1 - (u - v),
        even2 + db,
        odd3 + (u + v),
    ]


def fourier_kernel(in_hbm, table_ref, out_ref, got, low, waves, out, in_ref, sem):
    fetch(in_hbm, in_ref, sem)
    for d in range(Z):
        got[d * GR : (d + 1) * GR, :] = in_ref[d].astype(F32)
    lane = lanes(20)
    mains = [[], []]
    packed = [[], []]
    for h in range(2):
        mains[h] = eight([got[(2 * p + h) * GR : (2 * p + h) * GR + 80, :] for p in range(8)])
        packed[h] = eight([got[(2 * p + h) * GR + 80 : (2 * p + h) * GR + 100, :] for p in range(8)])
    for i in range(4):
        parts = [packed[pos % 2][i][pos // 2] for pos in range(4)]
        for e in range(4):
            v = roll(parts[0], -32 * e)
            for pos in range(1, 4):
                v = jnp.where(lane >= 32 * pos, roll(parts[pos], 32 * (pos - e)), v)
            low[10 * e : 10 * e + 10, :] = v[0:10]
            low[40 + 10 * e : 50 + 10 * e, :] = v[10:20]
        left = jnp.concatenate(
            [mains[0][i][0], mains[1][i][0], mains[0][i][1], mains[1][i][1], low[0:80, :]], axis=1
        ).astype(BF16)
        left = jnp.concatenate([left, jnp.zeros((48, 640), BF16)], axis=0)
        result = dot(table_ref[i], left, 1, 1)
        for m, w in enumerate((i, 8 - i) if i else (0, 4)):
            waves[w * 160 : w * 160 + 160, :] = result[m * 160 : m * 160 + 160]
    lane = lanes(Z)
    for row in range(WR):
        parts, c2 = row_pieces(row)
        v = None
        for k, q in enumerate(parts):
            piece = roll(waves[q * Z : q * Z + Z, :], 40 * (k - c2))
            v = piece if v is None else jnp.where(lane >= 40 * k, piece, v)
        out[pl.ds(row, Z, stride=WR), :] = v
    for d in range(Z):
        out_ref[d] = out[d * WR : (d + 1) * WR, :].astype(BF16)


def legendre_kernel(in_hbm, turned_hbm, out_hbm, got, three, block, turned, out, come, go, in_ref, sem):
    first = pltpu.make_async_copy(in_hbm, in_ref, sem)
    first.start()
    copies = [
        pltpu.make_async_copy(turned_hbm.at[pl.ds(4 * n, 4)], turned.at[pl.ds(4 * n, 4)], come.at[n])
        for n in range(5)
    ]
    for copy in copies:
        copy.start()
    first.wait()
    for d in range(Z):
        got[d * WR : (d + 1) * WR, :] = in_ref[d].astype(F32)
    zero = jnp.zeros((128, 128), BF16)
    gap = jnp.zeros((24, 128), F32)
    low = lanes(L) < 64
    for p3 in range(7):
        for row in range(8):
            three[p3, row * Z : row * Z + Z, :] = got[pl.ds(p3 * 8 + row, Z, stride=WR), :]
        v3 = three[p3].T
        for p in range(3 * p3, min(3 * p3 + 3, SP)):
            v = v3[(p % 3) * L : (p % 3) * L + L]
            both = jnp.concatenate([jnp.where(low, v, 0.0), gap, jnp.where(low, 0.0, v), gap], axis=0)
            here, there = 128 * (p % 2), 128 - 128 * (p % 2)
            block[p // 2, here : here + 128, here : here + 128] = both.astype(BF16)
            block[p // 2, here : here + 128, there : there + 128] = zero
    stores = []
    for step in range(5):
        copies[step].wait()
        results = []
        for g in (2 * step, 2 * step + 1):
            left = jnp.concatenate([turned[2 * g], turned[2 * g + 1]], axis=1)
            results.append(dot(left, block[g], 1, 0))
        for n in range(32):
            rows = []
            for result in results:
                even, odd = result[24 * n : 24 * n + 24, 0:128], result[24 * n : 24 * n + 24, 128:256]
                rows += [even[0:16], even[16:24] + odd[0:8], odd[8:24]]
            place = n % 8 * 4 + n // 8
            out[place, 80 * step : 80 * step + 80, :] = jnp.concatenate(rows, axis=0).astype(BF16)
        part = pl.ds(80 * step, 80)
        stores.append(pltpu.make_async_copy(out.at[:, part], out_hbm.at[:, part], go.at[step]))
        stores[-1].start()
    for copy in stores:
        copy.wait()


def parts_kernel(place_ref, in_ref, *out_refs):
    for d, out_ref in enumerate(out_refs):
        out_ref[...] = in_ref[pl.ds(pl.multiple_of((place_ref[0] + d) % 4 * 400, 16), 400), :]


def total_kernel(a_ref, b_ref, c_ref, d_ref, out_ref, total, split):
    parts = [ref[...].astype(F32) for ref in (a_ref, b_ref, c_ref, d_ref)]
    total[...] = (parts[0] + parts[1]) + (parts[2] + parts[3])
    for j in range(JD):
        v = total[pl.ds(j, SP, stride=JD), :]
        split[pl.ds(j * S, SP, stride=2), :] = v
        split[pl.ds(j * S + 1, SP, stride=2), :] = roll(v, 64)
    for j in range(JD):
        out_ref[j] = split[j * S : (j + 1) * S, 0:64]


def legendre_back_kernel(seeds_hbm, masked_hbm, out_ref, three, out, seeds, masked, come, come2):
    copies, later = [], []
    for step in range(5):
        part, pairs = pl.ds(80 * step, 80), pl.ds(4 * step, 4)
        copies.append(pltpu.make_async_copy(seeds_hbm.at[:, part], seeds.at[:, part], come.at[step]))
        later.append(pltpu.make_async_copy(masked_hbm.at[pairs], masked.at[pairs], come2.at[step]))
        copies[-1].start()
        later[-1].start()
    three[...] = jnp.zeros_like(three)
    low = lanes(L) < 64
    for step in range(5):
        copies[step].wait()
        later[step].wait()
        values = [seeds[n, 80 * step : 80 * step + 80, :].astype(F32) for n in range(32)]
        for g in (2 * step, 2 * step + 1):
            at = g % 2 * 40
            even = jnp.concatenate([v[at : at + 24] for v in values], axis=0).astype(BF16)
            odd = jnp.concatenate([v[at + 16 : at + 40] for v in values], axis=0).astype(BF16)
            right = jnp.concatenate([even, odd], axis=1)
            left = jnp.concatenate([masked[2 * g], masked[2 * g + 1]], axis=0)
            result = dot(left, right, 1, 0)
            for t in range(2):
                p = 2 * g + t
                both = result[80 * t : 80 * t + 80, 128 * t : 128 * t + 128]
                three[p // 3, p % 3 * L : p % 3 * L + L, :] = jnp.where(low, both[0:L], both[L : 2 * L])
    for p3 in range(7):
        v = three[p3].T
        for row in range(8):
            out[pl.ds(p3 * 8 + row, Z, stride=WR), :] = v[row * Z : row * Z + Z]
    for d in range(Z):
        out_ref[d] = out[d * WR : (d + 1) * WR, :].astype(BF16)


def fourier_back_kernel(in_hbm, table_ref, out_ref, got, waves, rests, out, in_ref, sem):
    fetch(in_hbm, in_ref, sem)
    for d in range(Z):
        got[d * WR : (d + 1) * WR, :] = in_ref[d].astype(F32)
    lane = lanes(Z)

    def piece(q, c2):
        row, place = wave_piece(q, c2)
        return roll(got[pl.ds(row, Z, stride=WR), :], 40 * (c2 - place))

    for i in range(8):
        p, m = (i % 4, i // 4) if i % 4 == 0 else (min(i, 8 - i), int(i > 4))
        for r in range(2):
            for b in range(BB):
                q = (i * 2 + r) * BB + b
                v = jnp.where(lane < 40, piece(q, 0), piece(q, 1))
                v = jnp.where(lane < 80, v, 0.0)
                at = p * 384 + (m * 2 + r) * NB + b * Z
                waves[at : at + Z, :] = v
    pairs = []
    for p in range(4):
        waves[p * 384 + 320 : p * 384 + 384, :] = jnp.zeros((64, 128), F32)
        left = jnp.concatenate(
            [waves[p * 384 + 128 * t : p * 384 + 128 * t + 128, :].T for t in range(3)], axis=1
        )
        left = left[0:80, 0:320].astype(BF16)
        pairs.append(dot(left, table_ref[p], 1, 0))
    for h in range(2):
        mains = [(v[:, 128 * h : 128 * h + 128], v[:, 256 + 128 * h : 384 + 128 * h]) for v in pairs]
        for p, v in enumerate(eight_back(mains)):
            out[(2 * p + h) * GR : (2 * p + h) * GR + 80, :] = v
    lane = lanes(20)
    for p in range(4):
        rests[p * 80 : p * 80 + 80, :] = pairs[p][:, 512:640]
    for h in range(2):
        packed = []
        for p in range(4):
            halves = []
            for part in range(2):
                pos = part * 2 + h
                v = None
                for e in range(4):
                    at = p * 80 + 10 * e
                    rows = jnp.concatenate([rests[at : at + 10, :], rests[at + 40 : at + 50, :]], axis=0)
                    rows = roll(rows, 32 * (e - pos))
                    v = rows if v is None else jnp.where(lane >= 32 * e, rows, v)
                halves.append(v)
            packed.append(tuple(halves))
        for p, v in enumerate(eight_back(packed)):
            out[(2 * p + h) * GR + 80 : (2 * p + h) * GR + 100, :] = v
    for d in range(Z):
        out_ref[d] = out[d * GR : (d + 1) * GR, :].astype(BF16)


def prep_basis(own, basis):
    return call(
        prep_basis_kernel,
        "prep_basis",
        (shape((SP, 2 * L, JW)), shape((SP, JW, 128))),
        [
            pltpu.VMEM((5, L * S, 128), F32),
            pltpu.VMEM((2, 5, 128, 128), F32),
            pltpu.VMEM((2, J, 128), F32),
            pltpu.VMEM((2, JW, 128), F32),
        ],
        smem=1,
        vmem=VMEM_ALL,
    )(own, basis)


def prep_table(block_slot):
    slots = jnp.arange(NB, dtype=jnp.int32)
    holder = jnp.sum(jnp.where(block_slot[None, :] == slots[:, None], slots[None, :], 0), axis=1)
    holder = holder.astype(jnp.int32)
    lane = np.arange(128)
    k = np.concatenate((lane, 160 + lane, 160 * (lane % 64 // 32) + 128 + lane % 32)).astype(np.int32)
    order = holder.reshape(Z, BB).T.reshape(NB)
    phase = (order[:, None] * k[None, :]) % 320
    angle = phase.astype(F32) * (2.0 * math.pi / 320)
    fine = 2.0 * math.pi * np.arange(8)[:, None] * k[None, :] / NLON
    scale = 1.0 / math.sqrt(NLON)
    ci = jnp.asarray((np.cos(fine) * scale).astype(np.float32))
    si = jnp.asarray((np.sin(fine) * scale).astype(np.float32))
    table = call(
        prep_table_kernel, "prep_table", shape((4, 320, 640)), []
    )(jnp.cos(angle), jnp.sin(angle), ci, si)
    return holder, table


def column_step(fields, weight_in, weight_out_t, seeds):
    return call(
        column_kernel,
        "column",
        (shape((Z, GR, 128)), shape((C, L * K)), shape((JD * SP, 128))),
        [
            pltpu.VMEM((C * L, 128), F32),
            pltpu.VMEM((C * L, 128), F32),
            pltpu.VMEM((Z * GR, 128), F32),
            pltpu.VMEM((JD * S, 128), F32),
            pltpu.VMEM((JD * SP, 128), F32),
        ],
        vmem=VMEM_ALL,
    )(fields, weight_in, weight_out_t, seeds)


def slope(keep, weight_in):
    return call(slope_kernel, "slope", shape((H, L * K)), [])(keep, weight_in)


def column_back(slopes, chunks, weight_in, weight_out_t):
    return call(
        column_back_kernel,
        "column_back",
        shape((C, L, K)),
        [
            pltpu.VMEM((C * L, 128), F32),
            pltpu.VMEM((C * L, 128), F32),
            pltpu.VMEM((Z * GR, 128), F32),
            pltpu.VMEM((C, 640), F32),
            pltpu.VMEM((H, L * K), BF16),
            pltpu.SemaphoreType.DMA((10,)),
            *fetched(Z, GR, 128),
        ],
        hbm=(0, 1),
    )(slopes, chunks, weight_in, weight_out_t)


def fourier(chunks, table):
    return call(
        fourier_kernel,
        "fourier",
        shape((Z, WR, 128)),
        [
            pltpu.VMEM((Z * GR, 128), F32),
            pltpu.VMEM((80, 128), F32),
            pltpu.VMEM((2 * M, 128), F32),
            pltpu.VMEM((Z * WR, 128), F32),
            *fetched(Z, GR, 128),
        ],
        hbm=(0,),
    )(chunks, table)


def fourier_back(chunks, table):
    return call(
        fourier_back_kernel,
        "fourier_back",
        shape((Z, GR, 128)),
        [
            pltpu.VMEM((Z * WR, 128), F32),
            pltpu.VMEM((4 * 384, 128), F32),
            pltpu.VMEM((320, 128), F32),
            pltpu.VMEM((Z * GR, 128), F32),
            *fetched(Z, WR, 128),
        ],
        hbm=(0,),
    )(chunks, table)


def legendre(chunks, turned):
    return call(
        legendre_kernel,
        "legendre",
        shape((32, JD * SP, 128)),
        [
            pltpu.VMEM((Z * WR, 128), F32),
            pltpu.VMEM((7, 128, 128), F32),
            pltpu.VMEM((S // 4, 256, 256), BF16),
            pltpu.VMEM((SP, JW, 128), BF16),
            pltpu.VMEM((32, JD * SP, 128), BF16),
            pltpu.SemaphoreType.DMA((5,)),
            pltpu.SemaphoreType.DMA((5,)),
            *fetched(Z, WR, 128),
        ],
        hbm=(0, 1),
        out_hbm=True,
        vmem=VMEM_ALL,
    )(chunks, turned)


def chip_parts(place, sums):
    return call(parts_kernel, "chip_parts", (shape((400, 128)),) * 4, [], smem=1)(place, sums)


def total(parts):
    return call(
        total_kernel,
        "total",
        shape((JD, S, 2 * C), F32),
        [pltpu.VMEM((JD * SP, 128), F32), pltpu.VMEM((JD * S, 128), F32)],
    )(*parts)


def legendre_back(seeds, masked):
    return call(
        legendre_back_kernel,
        "legendre_back",
        shape((Z, WR, 128)),
        [
            pltpu.VMEM((7, 128, 128), F32),
            pltpu.VMEM((Z * WR, 128), F32),
            pltpu.VMEM((32, JD * SP, 128), BF16),
            pltpu.VMEM((SP, 2 * L, JW), BF16),
            pltpu.SemaphoreType.DMA((5,)),
            pltpu.SemaphoreType.DMA((5,)),
        ],
        hbm=(0, 1),
        vmem=VMEM_ALL,
    )(seeds.reshape(32, JD * SP, 128), masked)


def exchange(values):
    return lax.all_to_all(values, "lon", split_axis=0, concat_axis=0, tiled=True)


def position(axis):
    return lax.axis_index(axis).astype(jnp.int32).reshape(1)


def after(values, earlier):
    return lax.optimization_barrier((values, earlier))[0]


def along(parts, axis):
    return [parts[0]] + [
        lax.ppermute(parts[d], axis, [(i, (i + d) % 4) for i in range(4)]) for d in (2, 1, 3)
    ]


def local(grid_fields, weight_in, weight_out, legendre_basis, block_slot, spectrum_grad):
    weight_out_t = weight_out.T
    chunks, keep, seeds = column_step(grid_fields, weight_in, weight_out_t, spectrum_grad)
    seeds = lax.all_gather(seeds, ("y", "x", "core"), axis=0, tiled=True)
    chunks, block_slot, legendre_basis = lax.optimization_barrier((chunks, block_slot, legendre_basis))
    chunks = exchange(chunks)
    holder, table = prep_table(block_slot)
    own = lax.dynamic_slice_in_dim(holder, lax.axis_index("lon") * BB, BB)
    masked, turned = prep_basis(own, legendre_basis)
    waves = exchange(fourier(chunks, table))
    sums = legendre(waves, turned)
    back = legendre_back(seeds, after(masked, sums))
    sums = lax.psum_scatter(sums.reshape(J * SP, 128), ("x", "core"), scatter_dimension=0, tiled=True)
    chunks = fourier_back(exchange(back), table)
    slopes = slope(after(keep, chunks), weight_in)
    parts = along(chip_parts(position("y"), after(sums, slopes)), "y")
    fields_grad = column_back(slopes, exchange(chunks), weight_in, weight_out_t)
    spectrum = total(parts)
    return (spectrum, fields_grad)


def solution(mesh):
    split = Mesh(mesh.devices.reshape(4, 4, 2, Z), ("y", "x", "core", "lon"))
    lat = ("y", "x", "core")
    in_specs = (P(None, lat, "lon"), P(), P(), P(lat, "lon", None), P(), P(lat, "lon", None))
    out_specs = (P(lat, "lon", None), P(None, lat, "lon"))
    return jax.shard_map(local, mesh=split, in_specs=in_specs, out_specs=out_specs, check_vma=False)
```

```python
import math

import jax
import jax.numpy as jnp
import numpy as np
from jax import lax
from jax.experimental import pallas as pl
from jax.experimental.pallas import tpu as pltpu
from jax.sharding import Mesh
from jax.sharding import PartitionSpec as P

NLON = 2560
M = 640
F32 = jnp.float32
BF16 = jnp.bfloat16

C = 32
H = 256
L = 40
K = 160
Z = 16
S = 40
J = 640
JD = 20
SP = S // 2
BB = 5
NB = 80
GR = 104
WR = 56
JW = 32 * 24
VMEM = 40 * 1024 * 1024
VMEM_ALL = 60 * 1024 * 1024


def dot(a, b, da, db):
    return lax.dot_general(a, b, (((da,), (db,)), ((), ())), preferred_element_type=F32)


def lanes(rows):
    return lax.broadcasted_iota(jnp.int32, (rows, 128), 1)


def grid_row(c2, t):
    return c2 * 40 + t if t < 40 else 80 + c2 * 10 + t - 40


def wave_piece(q, c2):
    i, r, b = q // (2 * BB), q // BB % 2, q % BB
    s = b * 8 + i
    return s // 6 * 8 + s % 2 * 4 + r * 2 + c2, s // 2 % 3


def row_pieces(row):
    slots = [row // 8 * 6 + 2 * k + row // 4 % 2 for k in range(3)]
    return [(s % 8 * 2 + row // 2 % 2) * BB + s // 8 for s in slots if s < S], row % 2


def roll(v, shift):
    shift = shift % 128
    return v if shift == 0 else pltpu.roll(v, shift, 1)


def call(kernel, name, out_shape, scratch, smem=0, hbm=(), out_hbm=False, vmem=VMEM):
    def run(*args):
        specs = [
            pl.BlockSpec(memory_space=pltpu.SMEM if i < smem else pl.ANY if i in hbm else pltpu.VMEM)
            for i in range(len(args))
        ]
        one = not isinstance(out_shape, (tuple, list))
        outs = pl.BlockSpec(memory_space=pl.ANY if out_hbm else pltpu.VMEM)
        return pl.pallas_call(
            kernel,
            name=name,
            out_shape=out_shape,
            in_specs=specs,
            out_specs=outs if one else tuple(outs for _ in out_shape),
            scratch_shapes=scratch,
            compiler_params=pltpu.CompilerParams(vmem_limit_bytes=vmem),
            cost_estimate=pl.CostEstimate(flops=1_000_000, bytes_accessed=100_000, transcendentals=0),
        )(*args)

    return run


def fetch(source, target, sem):
    copy = pltpu.make_async_copy(source, target, sem)
    copy.start()
    copy.wait()


def fetched(*dims):
    return [pltpu.VMEM(dims, BF16), pltpu.SemaphoreType.DMA]


def shape(dims, dtype=BF16):
    return jax.ShapeDtypeStruct(dims, dtype)


def prep_basis_kernel(own_ref, basis_ref, masked_ref, turned_ref, bs, tmp, column, wide):
    for row in range(L):
        v = basis_ref[row].astype(F32)
        for t in range(5):
            bs[t, row * S : (row + 1) * S, :] = v[:, 128 * t : 128 * t + 128]
    tmp[...] = jnp.zeros_like(tmp)
    wide[...] = jnp.zeros_like(wide)
    lane = lanes(L)

    def two_pairs(g, carry):
        for odd in range(2):
            p = 2 * g + odd
            for t in range(5):
                for e in range(2):
                    s = 2 * p + e
                    wave = own_ref[s // 8] * 8 + s % 8
                    v = bs[t, pl.ds(s, L, stride=S), :]
                    tmp[odd, t, 64 * e : 64 * e + L, :] = jnp.where(lane + 128 * t + wave <= M - 1, v, 0.0)
                column[odd, 128 * t : 128 * t + 128, :] = tmp[odd, t].T
            for n in range(32):
                at = 24 * n + 4 * odd
                wide[odd, at : at + JD, :] = column[odd, JD * n : JD * n + JD, :]
            turned_ref[p] = wide[odd].astype(BF16)
            for t in range(6):
                v = wide[odd, 128 * t : 128 * t + 128, :].T
                both = jnp.concatenate([v[0:L], v[64 : 64 + L]], axis=0).astype(BF16)
                masked_ref[p, :, 128 * t : 128 * t + 128] = both
        return carry

    lax.fori_loop(0, SP // 2, two_pairs, 0)


def prep_table_kernel(cb_ref, sb_ref, ci_ref, si_ref, table_ref):
    low = lanes(NB) < 64

    def angle(i, t):
        cb, sb = cb_ref[:, 128 * t : 128 * t + 128], sb_ref[:, 128 * t : 128 * t + 128]
        ci, si = ci_ref[i : i + 1, 128 * t : 128 * t + 128], si_ref[i : i + 1, 128 * t : 128 * t + 128]
        return cb * ci - sb * si, sb * ci + cb * si

    for p in range(4):
        for m, i in enumerate((p, 8 - p) if p else (0, 4)):
            for t in range(3):
                c, s = angle(i, t)
                zero = jnp.zeros_like(c)
                if p == 0:
                    first, second = (c, -s), (zero, zero)
                    if m == 1:
                        first, second = second, first
                elif m == 0:
                    first, second = (c, -s), (s, c)
                else:
                    first, second = (c, -s), (-s, -c)
                for r in range(2):
                    rows = slice((m * 2 + r) * NB, (m * 2 + r + 1) * NB)
                    if t < 2:
                        table_ref[p, rows, 128 * t : 128 * t + 128] = first[r].astype(BF16)
                        table_ref[p, rows, 256 + 128 * t : 384 + 128 * t] = second[r].astype(BF16)
                    else:
                        both = jnp.where(low, first[r], second[r])
                        table_ref[p, rows, 512:640] = both.astype(BF16)


def column_kernel(x_ref, win_ref, wout_ref, seeds_ref, out_ref, keep_ref, pack_ref, main, rest, out, rows, packed):
    for j in range(JD):
        rows[j * S : (j + 1) * S, 0:64] = seeds_ref[j].astype(F32)
    low = lanes(JD) < 64
    for p in range(SP):
        even, odd = rows[pl.ds(2 * p, JD, stride=S), :], rows[pl.ds(2 * p + 1, JD, stride=S), :]
        packed[p * JD : (p + 1) * JD, :] = jnp.where(low, even, roll(odd, 64))
    pack_ref[...] = packed[...].astype(BF16)
    for c in range(C):
        v = x_ref[c].astype(F32)
        main[c * L : (c + 1) * L, :] = v[:, :128]
        rest[c * L : (c + 1) * L, 0:32] = v[:, 128:K]
    lane = lanes(C)
    for t in range(50):
        if t < 40:
            v = main[pl.ds(t, C, stride=L), :]
        else:
            v = rest[pl.ds(t - 40, C, stride=L), :]
            for e in range(1, 4):
                v = jnp.where(lane >= 32 * e, roll(rest[pl.ds(t - 40 + 10 * e, C, stride=L), :], 32 * e), v)
        keep_ref[:, 128 * t : 128 * t + 128] = v.astype(BF16)
    win, wout = win_ref[...], wout_ref[...]
    for chunk in range(10):
        x = keep_ref[:, 640 * chunk : 640 * chunk + 640]
        pre = dot(win, x, 0, 0)
        half = 0.5 * pre
        active = (half + half * jnp.tanh(half)).astype(BF16)
        y = x.astype(F32) + dot(wout, active, 1, 0)
        for k in range(5):
            for c2 in range(2):
                row = grid_row(c2, 5 * chunk + k)
                out[pl.ds(row, Z, stride=GR), :] = y[Z * c2 : Z * c2 + Z, 128 * k : 128 * k + 128]
    for d in range(Z):
        out_ref[d] = out[d * GR : (d + 1) * GR, :].astype(BF16)


def slope_kernel(keep_ref, win_ref, out_ref):
    win = win_ref[...]
    for chunk in range(10):
        part = slice(640 * chunk, 640 * chunk + 640)
        pre = dot(win, keep_ref[:, part], 0, 0)
        sigma = 0.5 + 0.5 * jnp.tanh(0.5 * pre)
        out_ref[:, part] = (sigma * (1.0 + pre * (1.0 - sigma))).astype(BF16)


def column_back_kernel(slope_hbm, g_hbm, win_ref, wout_ref, out_ref, main, rest, got, up, slope, come, g_ref, sem):
    first = pltpu.make_async_copy(g_hbm, g_ref, sem)
    first.start()
    copies = []
    for chunk in range(10):
        part = pl.ds(640 * chunk, 640)
        copies.append(pltpu.make_async_copy(slope_hbm.at[:, part], slope.at[:, part], come.at[chunk]))
        copies[-1].start()
    first.wait()
    for d in range(Z):
        got[d * GR : (d + 1) * GR, :] = g_ref[d].astype(F32)
    win, wout = win_ref[...], wout_ref[...]
    for chunk in range(10):
        for k in range(5):
            t = 5 * chunk + k
            for c2 in range(2):
                up[Z * c2 : Z * c2 + Z, 128 * k : 128 * k + 128] = got[pl.ds(grid_row(c2, t), Z, stride=GR), :]
        upstream = up[...]
        act_grad = dot(wout, upstream.astype(BF16), 0, 0)
        copies[chunk].wait()
        pre_grad = (act_grad * slope[:, 640 * chunk : 640 * chunk + 640].astype(F32)).astype(BF16)
        y = upstream + dot(win, pre_grad, 1, 0)
        for k in range(5):
            t = 5 * chunk + k
            v = y[:, 128 * k : 128 * k + 128]
            if t < 40:
                main[pl.ds(t, C, stride=L), :] = v
            else:
                for e in range(4):
                    rest[pl.ds(t - 40 + 10 * e, C, stride=L), :] = roll(v, -32 * e)
    for c in range(C):
        out_ref[c, :, 0:128] = main[c * L : (c + 1) * L, :].astype(BF16)
        out_ref[c, :, 128:K] = rest[c * L : (c + 1) * L, 0:32].astype(BF16)


def eight(x):
    root = math.sqrt(0.5)
    s = [x[p] + x[p + 4] for p in range(4)]
    d = [x[p] - x[p + 4] for p in range(4)]
    e0, e1, o0, o1 = s[0] + s[2], s[0] - s[2], s[1] + s[3], s[1] - s[3]
    u, v = root * (d[1] - d[3]), root * (d[1] + d[3])
    return [(e0 + o0, e0 - o0), (d[0] + u, -d[2] - v), (e1, -o1), (d[0] - u, d[2] - v)]


def eight_back(pairs):
    root = math.sqrt(0.5)
    (a0, b0), (a1, b1), (a2, b2), (a3, b3) = pairs
    plus, minus = a0 + b0, a0 - b0
    sa, da, sb, db = a1 + a3, a1 - a3, b1 + b3, b1 - b3
    even0, even2 = plus + a2, plus - a2
    odd1, odd3 = minus - b2, minus + b2
    u, v = root * da, root * sb
    return [
        even0 + sa,
        odd1 + (u - v),
        even2 - db,
        odd3 - (u + v),
        even0 - sa,
        odd1 - (u - v),
        even2 + db,
        odd3 + (u + v),
    ]


def fourier_kernel(in_hbm, table_ref, out_ref, got, low, waves, out, in_ref, sem):
    fetch(in_hbm, in_ref, sem)
    for d in range(Z):
        got[d * GR : (d + 1) * GR, :] = in_ref[d].astype(F32)
    lane = lanes(20)
    mains = [[], []]
    packed = [[], []]
    for h in range(2):
        mains[h] = eight([got[(2 * p + h) * GR : (2 * p + h) * GR + 80, :] for p in range(8)])
        packed[h] = eight([got[(2 * p + h) * GR + 80 : (2 * p + h) * GR + 100, :] for p in range(8)])
    for i in range(4):
        parts = [packed[pos % 2][i][pos // 2] for pos in range(4)]
        for e in range(4):
            v = roll(parts[0], -32 * e)
            for pos in range(1, 4):
                v = jnp.where(lane >= 32 * pos, roll(parts[pos], 32 * (pos - e)), v)
            low[10 * e : 10 * e + 10, :] = v[0:10]
            low[40 + 10 * e : 50 + 10 * e, :] = v[10:20]
        left = jnp.concatenate(
            [mains[0][i][0], mains[1][i][0], mains[0][i][1], mains[1][i][1], low[0:80, :]], axis=1
        ).astype(BF16)
        left = jnp.concatenate([left, jnp.zeros((48, 640), BF16)], axis=0)
        result = dot(table_ref[i], left, 1, 1)
        for m, w in enumerate((i, 8 - i) if i else (0, 4)):
            waves[w * 160 : w * 160 + 160, :] = result[m * 160 : m * 160 + 160]
    lane = lanes(Z)
    for row in range(WR):
        parts, c2 = row_pieces(row)
        v = None
        for k, q in enumerate(parts):
            piece = roll(waves[q * Z : q * Z + Z, :], 40 * (k - c2))
            v = piece if v is None else jnp.where(lane >= 40 * k, piece, v)
        out[pl.ds(row, Z, stride=WR), :] = v
    for d in range(Z):
        out_ref[d] = out[d * WR : (d + 1) * WR, :].astype(BF16)


def legendre_kernel(in_hbm, turned_hbm, out_hbm, got, three, block, turned, out, come, go, in_ref, sem):
    first = pltpu.make_async_copy(in_hbm, in_ref, sem)
    first.start()
    copies = [
        pltpu.make_async_copy(turned_hbm.at[pl.ds(4 * n, 4)], turned.at[pl.ds(4 * n, 4)], come.at[n])
        for n in range(5)
    ]
    for copy in copies:
        copy.start()
    first.wait()
    for d in range(Z):
        got[d * WR : (d + 1) * WR, :] = in_ref[d].astype(F32)
    zero = jnp.zeros((128, 128), BF16)
    gap = jnp.zeros((24, 128), F32)
    low = lanes(L) < 64
    for p3 in range(7):
        for row in range(8):
            three[p3, row * Z : row * Z + Z, :] = got[pl.ds(p3 * 8 + row, Z, stride=WR), :]
        v3 = three[p3].T
        for p in range(3 * p3, min(3 * p3 + 3, SP)):
            v = v3[(p % 3) * L : (p % 3) * L + L]
            both = jnp.concatenate([jnp.where(low, v, 0.0), gap, jnp.where(low, 0.0, v), gap], axis=0)
            here, there = 128 * (p % 2), 128 - 128 * (p % 2)
            block[p // 2, here : here + 128, here : here + 128] = both.astype(BF16)
            block[p // 2, here : here + 128, there : there + 128] = zero
    stores = []
    for step in range(5):
        copies[step].wait()
        results = []
        for g in (2 * step, 2 * step + 1):
            left = jnp.concatenate([turned[2 * g], turned[2 * g + 1]], axis=1)
            results.append(dot(left, block[g], 1, 0))
        for n in range(32):
            rows = []
            for result in results:
                even, odd = result[24 * n : 24 * n + 24, 0:128], result[24 * n : 24 * n + 24, 128:256]
                rows += [even[0:16], even[16:24] + odd[0:8], odd[8:24]]
            place = n % 8 * 4 + n // 8
            out[place, 80 * step : 80 * step + 80, :] = jnp.concatenate(rows, axis=0).astype(BF16)
        part = pl.ds(80 * step, 80)
        stores.append(pltpu.make_async_copy(out.at[:, part], out_hbm.at[:, part], go.at[step]))
        stores[-1].start()
    for copy in stores:
        copy.wait()


def parts_kernel(place_ref, in_ref, *out_refs):
    for d, out_ref in enumerate(out_refs):
        out_ref[...] = in_ref[pl.ds(pl.multiple_of((place_ref[0] + d) % 4 * 400, 16), 400), :]


def total_kernel(a_ref, b_ref, c_ref, d_ref, out_ref, total, split):
    parts = [ref[...].astype(F32) for ref in (a_ref, b_ref, c_ref, d_ref)]
    total[...] = (parts[0] + parts[1]) + (parts[2] + parts[3])
    for j in range(JD):
        v = total[pl.ds(j, SP, stride=JD), :]
        split[pl.ds(j * S, SP, stride=2), :] = v
        split[pl.ds(j * S + 1, SP, stride=2), :] = roll(v, 64)
    for j in range(JD):
        out_ref[j] = split[j * S : (j + 1) * S, 0:64]


def legendre_back_kernel(seeds_hbm, masked_hbm, out_ref, three, out, seeds, masked, come, come2):
    copies, later = [], []
    for step in range(5):
        part, pairs = pl.ds(80 * step, 80), pl.ds(4 * step, 4)
        copies.append(pltpu.make_async_copy(seeds_hbm.at[:, part], seeds.at[:, part], come.at[step]))
        later.append(pltpu.make_async_copy(masked_hbm.at[pairs], masked.at[pairs], come2.at[step]))
        copies[-1].start()
        later[-1].start()
    three[...] = jnp.zeros_like(three)
    low = lanes(L) < 64
    for step in range(5):
        copies[step].wait()
        later[step].wait()
        values = [seeds[n, 80 * step : 80 * step + 80, :].astype(F32) for n in range(32)]
        for g in (2 * step, 2 * step + 1):
            at = g % 2 * 40
            even = jnp.concatenate([v[at : at + 24] for v in values], axis=0).astype(BF16)
            odd = jnp.concatenate([v[at + 16 : at + 40] for v in values], axis=0).astype(BF16)
            right = jnp.concatenate([even, odd], axis=1)
            left = jnp.concatenate([masked[2 * g], masked[2 * g + 1]], axis=0)
            result = dot(left, right, 1, 0)
            for t in range(2):
                p = 2 * g + t
                both = result[80 * t : 80 * t + 80, 128 * t : 128 * t + 128]
                three[p // 3, p % 3 * L : p % 3 * L + L, :] = jnp.where(low, both[0:L], both[L : 2 * L])
    for p3 in range(7):
        v = three[p3].T
        for row in range(8):
            out[pl.ds(p3 * 8 + row, Z, stride=WR), :] = v[row * Z : row * Z + Z]
    for d in range(Z):
        out_ref[d] = out[d * WR : (d + 1) * WR, :].astype(BF16)


def fourier_back_kernel(in_hbm, table_ref, out_ref, got, waves, rests, out, in_ref, sem):
    fetch(in_hbm, in_ref, sem)
    for d in range(Z):
        got[d * WR : (d + 1) * WR, :] = in_ref[d].astype(F32)
    lane = lanes(Z)

    def piece(q, c2):
        row, place = wave_piece(q, c2)
        return roll(got[pl.ds(row, Z, stride=WR), :], 40 * (c2 - place))

    for i in range(8):
        p, m = (i % 4, i // 4) if i % 4 == 0 else (min(i, 8 - i), int(i > 4))
        for r in range(2):
            for b in range(BB):
                q = (i * 2 + r) * BB + b
                v = jnp.where(lane < 40, piece(q, 0), piece(q, 1))
                v = jnp.where(lane < 80, v, 0.0)
                at = p * 384 + (m * 2 + r) * NB + b * Z
                waves[at : at + Z, :] = v
    pairs = []
    for p in range(4):
        waves[p * 384 + 320 : p * 384 + 384, :] = jnp.zeros((64, 128), F32)
        left = jnp.concatenate(
            [waves[p * 384 + 128 * t : p * 384 + 128 * t + 128, :].T for t in range(3)], axis=1
        )
        left = left[0:80, 0:320].astype(BF16)
        pairs.append(dot(left, table_ref[p], 1, 0))
    for h in range(2):
        mains = [(v[:, 128 * h : 128 * h + 128], v[:, 256 + 128 * h : 384 + 128 * h]) for v in pairs]
        for p, v in enumerate(eight_back(mains)):
            out[(2 * p + h) * GR : (2 * p + h) * GR + 80, :] = v
    lane = lanes(20)
    for p in range(4):
        rests[p * 80 : p * 80 + 80, :] = pairs[p][:, 512:640]
    for h in range(2):
        packed = []
        for p in range(4):
            halves = []
            for part in range(2):
                pos = part * 2 + h
                v = None
                for e in range(4):
                    at = p * 80 + 10 * e
                    rows = jnp.concatenate([rests[at : at + 10, :], rests[at + 40 : at + 50, :]], axis=0)
                    rows = roll(rows, 32 * (e - pos))
                    v = rows if v is None else jnp.where(lane >= 32 * e, rows, v)
                halves.append(v)
            packed.append(tuple(halves))
        for p, v in enumerate(eight_back(packed)):
            out[(2 * p + h) * GR + 80 : (2 * p + h) * GR + 100, :] = v
    for d in range(Z):
        out_ref[d] = out[d * GR : (d + 1) * GR, :].astype(BF16)


def prep_basis(own, basis):
    return call(
        prep_basis_kernel,
        "prep_basis",
        (shape((SP, 2 * L, JW)), shape((SP, JW, 128))),
        [
            pltpu.VMEM((5, L * S, 128), F32),
            pltpu.VMEM((2, 5, 128, 128), F32),
            pltpu.VMEM((2, J, 128), F32),
            pltpu.VMEM((2, JW, 128), F32),
        ],
        smem=1,
        vmem=VMEM_ALL,
    )(own, basis)


def prep_table(block_slot):
    slots = jnp.arange(NB, dtype=jnp.int32)
    holder = jnp.sum(jnp.where(block_slot[None, :] == slots[:, None], slots[None, :], 0), axis=1)
    holder = holder.astype(jnp.int32)
    lane = np.arange(128)
    k = np.concatenate((lane, 160 + lane, 160 * (lane % 64 // 32) + 128 + lane % 32)).astype(np.int32)
    order = holder.reshape(Z, BB).T.reshape(NB)
    phase = (order[:, None] * k[None, :]) % 320
    angle = phase.astype(F32) * (2.0 * math.pi / 320)
    fine = 2.0 * math.pi * np.arange(8)[:, None] * k[None, :] / NLON
    scale = 1.0 / math.sqrt(NLON)
    ci = jnp.asarray((np.cos(fine) * scale).astype(np.float32))
    si = jnp.asarray((np.sin(fine) * scale).astype(np.float32))
    table = call(
        prep_table_kernel, "prep_table", shape((4, 320, 640)), []
    )(jnp.cos(angle), jnp.sin(angle), ci, si)
    return holder, table


def column_step(fields, weight_in, weight_out_t, seeds):
    return call(
        column_kernel,
        "column",
        (shape((Z, GR, 128)), shape((C, L * K)), shape((JD * SP, 128))),
        [
            pltpu.VMEM((C * L, 128), F32),
            pltpu.VMEM((C * L, 128), F32),
            pltpu.VMEM((Z * GR, 128), F32),
            pltpu.VMEM((JD * S, 128), F32),
            pltpu.VMEM((JD * SP, 128), F32),
        ],
        vmem=VMEM_ALL,
    )(fields, weight_in, weight_out_t, seeds)


def slope(keep, weight_in):
    return call(slope_kernel, "slope", shape((H, L * K)), [])(keep, weight_in)


def column_back(slopes, chunks, weight_in, weight_out_t):
    return call(
        column_back_kernel,
        "column_back",
        shape((C, L, K)),
        [
            pltpu.VMEM((C * L, 128), F32),
            pltpu.VMEM((C * L, 128), F32),
            pltpu.VMEM((Z * GR, 128), F32),
            pltpu.VMEM((C, 640), F32),
            pltpu.VMEM((H, L * K), BF16),
            pltpu.SemaphoreType.DMA((10,)),
            *fetched(Z, GR, 128),
        ],
        hbm=(0, 1),
    )(slopes, chunks, weight_in, weight_out_t)


def fourier(chunks, table):
    return call(
        fourier_kernel,
        "fourier",
        shape((Z, WR, 128)),
        [
            pltpu.VMEM((Z * GR, 128), F32),
            pltpu.VMEM((80, 128), F32),
            pltpu.VMEM((2 * M, 128), F32),
            pltpu.VMEM((Z * WR, 128), F32),
            *fetched(Z, GR, 128),
        ],
        hbm=(0,),
    )(chunks, table)


def fourier_back(chunks, table):
    return call(
        fourier_back_kernel,
        "fourier_back",
        shape((Z, GR, 128)),
        [
            pltpu.VMEM((Z * WR, 128), F32),
            pltpu.VMEM((4 * 384, 128), F32),
            pltpu.VMEM((320, 128), F32),
            pltpu.VMEM((Z * GR, 128), F32),
            *fetched(Z, WR, 128),
        ],
        hbm=(0,),
    )(chunks, table)


def legendre(chunks, turned):
    return call(
        legendre_kernel,
        "legendre",
        shape((32, JD * SP, 128)),
        [
            pltpu.VMEM((Z * WR, 128), F32),
            pltpu.VMEM((7, 128, 128), F32),
            pltpu.VMEM((S // 4, 256, 256), BF16),
            pltpu.VMEM((SP, JW, 128), BF16),
            pltpu.VMEM((32, JD * SP, 128), BF16),
            pltpu.SemaphoreType.DMA((5,)),
            pltpu.SemaphoreType.DMA((5,)),
            *fetched(Z, WR, 128),
        ],
        hbm=(0, 1),
        out_hbm=True,
        vmem=VMEM_ALL,
    )(chunks, turned)


def chip_parts(place, sums):
    return call(parts_kernel, "chip_parts", (shape((400, 128)),) * 4, [], smem=1)(place, sums)


def total(parts):
    return call(
        total_kernel,
        "total",
        shape((JD, S, 2 * C), F32),
        [pltpu.VMEM((JD * SP, 128), F32), pltpu.VMEM((JD * S, 128), F32)],
    )(*parts)


def legendre_back(seeds, masked):
    return call(
        legendre_back_kernel,
        "legendre_back",
        shape((Z, WR, 128)),
        [
            pltpu.VMEM((7, 128, 128), F32),
            pltpu.VMEM((Z * WR, 128), F32),
            pltpu.VMEM((32, JD * SP, 128), BF16),
            pltpu.VMEM((SP, 2 * L, JW), BF16),
            pltpu.SemaphoreType.DMA((5,)),
            pltpu.SemaphoreType.DMA((5,)),
        ],
        hbm=(0, 1),
        vmem=VMEM_ALL,
    )(seeds.reshape(32, JD * SP, 128), masked)


def exchange(values):
    return lax.all_to_all(values, "lon", split_axis=0, concat_axis=0, tiled=True)


def position(axis):
    return lax.axis_index(axis).astype(jnp.int32).reshape(1)


def after(values, earlier):
    return lax.optimization_barrier((values, earlier))[0]


def along(parts, axis):
    return [parts[0]] + [
        lax.ppermute(parts[d], axis, [(i, (i + d) % 4) for i in range(4)]) for d in (2, 1, 3)
    ]


def local(grid_fields, weight_in, weight_out, legendre_basis, block_slot, spectrum_grad):
    weight_out_t = weight_out.T
    chunks, keep, seeds = column_step(grid_fields, weight_in, weight_out_t, spectrum_grad)
    seeds = lax.all_gather(seeds, ("y", "x", "core"), axis=0, tiled=True)
    chunks, block_slot, legendre_basis = lax.optimization_barrier((chunks, block_slot, legendre_basis))
    chunks = exchange(chunks)
    holder, table = prep_table(block_slot)
    own = lax.dynamic_slice_in_dim(holder, lax.axis_index("lon") * BB, BB)
    masked, turned = prep_basis(own, legendre_basis)
    waves = exchange(fourier(chunks, table))
    sums = legendre(waves, turned)
    back = legendre_back(seeds, after(masked, sums))
    sums = lax.psum_scatter(sums.reshape(J * SP, 128), ("x", "core"), scatter_dimension=0, tiled=True)
    chunks = fourier_back(exchange(back), table)
    slopes = slope(after(keep, chunks), weight_in)
    parts = along(chip_parts(position("y"), after(sums, slopes)), "y")
    spectrum = total(parts)
    fields_grad = column_back(slopes, after(exchange(chunks), spectrum), weight_in, weight_out_t)
    return (spectrum, fields_grad)


def solution(mesh):
    split = Mesh(mesh.devices.reshape(4, 4, 2, Z), ("y", "x", "core", "lon"))
    lat = ("y", "x", "core")
    in_specs = (P(None, lat, "lon"), P(), P(), P(lat, "lon", None), P(), P(lat, "lon", None))
    out_specs = (P(lat, "lon", None), P(None, lat, "lon"))
    return jax.shard_map(local, mesh=split, in_specs=in_specs, out_specs=out_specs, check_vma=False)
```

```python
import math

import jax
import jax.numpy as jnp
import numpy as np
from jax import lax
from jax.experimental import pallas as pl
from jax.experimental.pallas import tpu as pltpu
from jax.sharding import Mesh
from jax.sharding import PartitionSpec as P

NLON = 2560
M = 640
F32 = jnp.float32
BF16 = jnp.bfloat16

C = 32
H = 256
L = 40
K = 160
Z = 16
S = 40
J = 640
JD = 20
SP = S // 2
BB = 5
NB = 80
GR = 104
WR = 56
JW = 32 * 24
VMEM = 40 * 1024 * 1024
VMEM_ALL = 60 * 1024 * 1024


def dot(a, b, da, db):
    return lax.dot_general(a, b, (((da,), (db,)), ((), ())), preferred_element_type=F32)


def lanes(rows):
    return lax.broadcasted_iota(jnp.int32, (rows, 128), 1)


def grid_row(c2, t):
    return c2 * 40 + t if t < 40 else 80 + c2 * 10 + t - 40


def wave_piece(q, c2):
    i, r, b = q // (2 * BB), q // BB % 2, q % BB
    s = b * 8 + i
    return s // 6 * 8 + s % 2 * 4 + r * 2 + c2, s // 2 % 3


def row_pieces(row):
    slots = [row // 8 * 6 + 2 * k + row // 4 % 2 for k in range(3)]
    return [(s % 8 * 2 + row // 2 % 2) * BB + s // 8 for s in slots if s < S], row % 2


def roll(v, shift):
    shift = shift % 128
    return v if shift == 0 else pltpu.roll(v, shift, 1)


def call(kernel, name, out_shape, scratch, smem=0, hbm=(), out_hbm=False, vmem=VMEM):
    def run(*args):
        specs = [
            pl.BlockSpec(memory_space=pltpu.SMEM if i < smem else pl.ANY if i in hbm else pltpu.VMEM)
            for i in range(len(args))
        ]
        one = not isinstance(out_shape, (tuple, list))
        outs = pl.BlockSpec(memory_space=pl.ANY if out_hbm else pltpu.VMEM)
        return pl.pallas_call(
            kernel,
            name=name,
            out_shape=out_shape,
            in_specs=specs,
            out_specs=outs if one else tuple(outs for _ in out_shape),
            scratch_shapes=scratch,
            compiler_params=pltpu.CompilerParams(vmem_limit_bytes=vmem),
            cost_estimate=pl.CostEstimate(flops=1_000_000, bytes_accessed=100_000, transcendentals=0),
        )(*args)

    return run


def fetch(source, target, sem):
    copy = pltpu.make_async_copy(source, target, sem)
    copy.start()
    copy.wait()


def fetched(*dims):
    return [pltpu.VMEM(dims, BF16), pltpu.SemaphoreType.DMA]


def shape(dims, dtype=BF16):
    return jax.ShapeDtypeStruct(dims, dtype)


def prep_basis_kernel(own_ref, basis_ref, masked_ref, turned_ref, bs, tmp, column, wide):
    for row in range(L):
        v = basis_ref[row].astype(F32)
        for t in range(5):
            bs[t, row * S : (row + 1) * S, :] = v[:, 128 * t : 128 * t + 128]
    tmp[...] = jnp.zeros_like(tmp)
    wide[...] = jnp.zeros_like(wide)
    lane = lanes(L)

    def two_pairs(g, carry):
        for odd in range(2):
            p = 2 * g + odd
            for t in range(5):
                for e in range(2):
                    s = 2 * p + e
                    wave = own_ref[s // 8] * 8 + s % 8
                    v = bs[t, pl.ds(s, L, stride=S), :]
                    tmp[odd, t, 64 * e : 64 * e + L, :] = jnp.where(lane + 128 * t + wave <= M - 1, v, 0.0)
                column[odd, 128 * t : 128 * t + 128, :] = tmp[odd, t].T
            for n in range(32):
                at = 24 * n + 4 * odd
                wide[odd, at : at + JD, :] = column[odd, JD * n : JD * n + JD, :]
            turned_ref[p] = wide[odd].astype(BF16)
            for t in range(6):
                v = wide[odd, 128 * t : 128 * t + 128, :].T
                both = jnp.concatenate([v[0:L], v[64 : 64 + L]], axis=0).astype(BF16)
                masked_ref[p, :, 128 * t : 128 * t + 128] = both
        return carry

    lax.fori_loop(0, SP // 2, two_pairs, 0)


def prep_table_kernel(cb_ref, sb_ref, ci_ref, si_ref, table_ref):
    low = lanes(NB) < 64

    def angle(i, t):
        cb, sb = cb_ref[:, 128 * t : 128 * t + 128], sb_ref[:, 128 * t : 128 * t + 128]
        ci, si = ci_ref[i : i + 1, 128 * t : 128 * t + 128], si_ref[i : i + 1, 128 * t : 128 * t + 128]
        return cb * ci - sb * si, sb * ci + cb * si

    for p in range(4):
        for m, i in enumerate((p, 8 - p) if p else (0, 4)):
            for t in range(3):
                c, s = angle(i, t)
                zero = jnp.zeros_like(c)
                if p == 0:
                    first, second = (c, -s), (zero, zero)
                    if m == 1:
                        first, second = second, first
                elif m == 0:
                    first, second = (c, -s), (s, c)
                else:
                    first, second = (c, -s), (-s, -c)
                for r in range(2):
                    rows = slice((m * 2 + r) * NB, (m * 2 + r + 1) * NB)
                    if t < 2:
                        table_ref[p, rows, 128 * t : 128 * t + 128] = first[r].astype(BF16)
                        table_ref[p, rows, 256 + 128 * t : 384 + 128 * t] = second[r].astype(BF16)
                    else:
                        both = jnp.where(low, first[r], second[r])
                        table_ref[p, rows, 512:640] = both.astype(BF16)


def column_kernel(x_ref, win_ref, wout_ref, seeds_ref, out_ref, keep_ref, pack_ref, main, rest, out, rows, packed):
    for j in range(JD):
        rows[j * S : (j + 1) * S, 0:64] = seeds_ref[j].astype(F32)
    low = lanes(JD) < 64
    for p in range(SP):
        even, odd = rows[pl.ds(2 * p, JD, stride=S), :], rows[pl.ds(2 * p + 1, JD, stride=S), :]
        packed[p * JD : (p + 1) * JD, :] = jnp.where(low, even, roll(odd, 64))
    pack_ref[...] = packed[...].astype(BF16)
    for c in range(C):
        v = x_ref[c].astype(F32)
        main[c * L : (c + 1) * L, :] = v[:, :128]
        rest[c * L : (c + 1) * L, 0:32] = v[:, 128:K]
    lane = lanes(C)
    for t in range(50):
        if t < 40:
            v = main[pl.ds(t, C, stride=L), :]
        else:
            v = rest[pl.ds(t - 40, C, stride=L), :]
            for e in range(1, 4):
                v = jnp.where(lane >= 32 * e, roll(rest[pl.ds(t - 40 + 10 * e, C, stride=L), :], 32 * e), v)
        keep_ref[:, 128 * t : 128 * t + 128] = v.astype(BF16)
    win, wout = win_ref[...], wout_ref[...]
    for chunk in range(10):
        x = keep_ref[:, 640 * chunk : 640 * chunk + 640]
        pre = dot(win, x, 0, 0)
        half = 0.5 * pre
        active = (half + half * jnp.tanh(half)).astype(BF16)
        y = x.astype(F32) + dot(wout, active, 1, 0)
        for k in range(5):
            for c2 in range(2):
                row = grid_row(c2, 5 * chunk + k)
                out[pl.ds(row, Z, stride=GR), :] = y[Z * c2 : Z * c2 + Z, 128 * k : 128 * k + 128]
    for d in range(Z):
        out_ref[d] = out[d * GR : (d + 1) * GR, :].astype(BF16)


def column_back_kernel(keep_ref, g_hbm, win_ref, wout_ref, out_ref, main, rest, got, up, g_ref, sem):
    fetch(g_hbm, g_ref, sem)
    for d in range(Z):
        got[d * GR : (d + 1) * GR, :] = g_ref[d].astype(F32)
    win, wout = win_ref[...], wout_ref[...]
    for chunk in range(10):
        for k in range(5):
            t = 5 * chunk + k
            for c2 in range(2):
                up[Z * c2 : Z * c2 + Z, 128 * k : 128 * k + 128] = got[pl.ds(grid_row(c2, t), Z, stride=GR), :]
        upstream = up[...]
        act_grad = dot(wout, upstream.astype(BF16), 0, 0)
        pre = dot(win, keep_ref[:, 640 * chunk : 640 * chunk + 640], 0, 0)
        sigma = 0.5 + 0.5 * jnp.tanh(0.5 * pre)
        pre_grad = (act_grad * (sigma * (1.0 + pre * (1.0 - sigma)))).astype(BF16)
        y = upstream + dot(win, pre_grad, 1, 0)
        for k in range(5):
            t = 5 * chunk + k
            v = y[:, 128 * k : 128 * k + 128]
            if t < 40:
                main[pl.ds(t, C, stride=L), :] = v
            else:
                for e in range(4):
                    rest[pl.ds(t - 40 + 10 * e, C, stride=L), :] = roll(v, -32 * e)
    for c in range(C):
        out_ref[c, :, 0:128] = main[c * L : (c + 1) * L, :].astype(BF16)
        out_ref[c, :, 128:K] = rest[c * L : (c + 1) * L, 0:32].astype(BF16)


def eight(x):
    root = math.sqrt(0.5)
    s = [x[p] + x[p + 4] for p in range(4)]
    d = [x[p] - x[p + 4] for p in range(4)]
    e0, e1, o0, o1 = s[0] + s[2], s[0] - s[2], s[1] + s[3], s[1] - s[3]
    u, v = root * (d[1] - d[3]), root * (d[1] + d[3])
    return [(e0 + o0, e0 - o0), (d[0] + u, -d[2] - v), (e1, -o1), (d[0] - u, d[2] - v)]


def eight_back(pairs):
    root = math.sqrt(0.5)
    (a0, b0), (a1, b1), (a2, b2), (a3, b3) = pairs
    plus, minus = a0 + b0, a0 - b0
    sa, da, sb, db = a1 + a3, a1 - a3, b1 + b3, b1 - b3
    even0, even2 = plus + a2, plus - a2
    odd1, odd3 = minus - b2, minus + b2
    u, v = root * da, root * sb
    return [
        even0 + sa,
        odd1 + (u - v),
        even2 - db,
        odd3 - (u + v),
        even0 - sa,
        odd1 - (u - v),
        even2 + db,
        odd3 + (u + v),
    ]


def fourier_kernel(in_hbm, table_ref, out_ref, got, low, waves, out, in_ref, sem):
    fetch(in_hbm, in_ref, sem)
    for d in range(Z):
        got[d * GR : (d + 1) * GR, :] = in_ref[d].astype(F32)
    lane = lanes(20)
    mains = [[], []]
    packed = [[], []]
    for h in range(2):
        mains[h] = eight([got[(2 * p + h) * GR : (2 * p + h) * GR + 80, :] for p in range(8)])
        packed[h] = eight([got[(2 * p + h) * GR + 80 : (2 * p + h) * GR + 100, :] for p in range(8)])
    for i in range(4):
        parts = [packed[pos % 2][i][pos // 2] for pos in range(4)]
        for e in range(4):
            v = roll(parts[0], -32 * e)
            for pos in range(1, 4):
                v = jnp.where(lane >= 32 * pos, roll(parts[pos], 32 * (pos - e)), v)
            low[10 * e : 10 * e + 10, :] = v[0:10]
            low[40 + 10 * e : 50 + 10 * e, :] = v[10:20]
        left = jnp.concatenate(
            [mains[0][i][0], mains[1][i][0], mains[0][i][1], mains[1][i][1], low[0:80, :]], axis=1
        ).astype(BF16)
        left = jnp.concatenate([left, jnp.zeros((48, 640), BF16)], axis=0)
        result = dot(table_ref[i], left, 1, 1)
        for m, w in enumerate((i, 8 - i) if i else (0, 4)):
            waves[w * 160 : w * 160 + 160, :] = result[m * 160 : m * 160 + 160]
    lane = lanes(Z)
    for row in range(WR):
        parts, c2 = row_pieces(row)
        v = None
        for k, q in enumerate(parts):
            piece = roll(waves[q * Z : q * Z + Z, :], 40 * (k - c2))
            v = piece if v is None else jnp.where(lane >= 40 * k, piece, v)
        out[pl.ds(row, Z, stride=WR), :] = v
    for d in range(Z):
        out_ref[d] = out[d * WR : (d + 1) * WR, :].astype(BF16)


def legendre_kernel(in_hbm, turned_hbm, out_hbm, got, three, block, turned, out, come, go, in_ref, sem):
    first = pltpu.make_async_copy(in_hbm, in_ref, sem)
    first.start()
    copies = [
        pltpu.make_async_copy(turned_hbm.at[pl.ds(4 * n, 4)], turned.at[pl.ds(4 * n, 4)], come.at[n])
        for n in range(5)
    ]
    for copy in copies:
        copy.start()
    first.wait()
    for d in range(Z):
        got[d * WR : (d + 1) * WR, :] = in_ref[d].astype(F32)
    zero = jnp.zeros((128, 128), BF16)
    gap = jnp.zeros((24, 128), F32)
    low = lanes(L) < 64
    for p3 in range(7):
        for row in range(8):
            three[p3, row * Z : row * Z + Z, :] = got[pl.ds(p3 * 8 + row, Z, stride=WR), :]
        v3 = three[p3].T
        for p in range(3 * p3, min(3 * p3 + 3, SP)):
            v = v3[(p % 3) * L : (p % 3) * L + L]
            both = jnp.concatenate([jnp.where(low, v, 0.0), gap, jnp.where(low, 0.0, v), gap], axis=0)
            here, there = 128 * (p % 2), 128 - 128 * (p % 2)
            block[p // 2, here : here + 128, here : here + 128] = both.astype(BF16)
            block[p // 2, here : here + 128, there : there + 128] = zero
    stores = []
    for step in range(5):
        copies[step].wait()
        results = []
        for g in (2 * step, 2 * step + 1):
            left = jnp.concatenate([turned[2 * g], turned[2 * g + 1]], axis=1)
            results.append(dot(left, block[g], 1, 0))
        for n in range(32):
            rows = []
            for result in results:
                even, odd = result[24 * n : 24 * n + 24, 0:128], result[24 * n : 24 * n + 24, 128:256]
                rows += [even[0:16], even[16:24] + odd[0:8], odd[8:24]]
            place = n % 8 * 4 + n // 8
            out[place, 80 * step : 80 * step + 80, :] = jnp.concatenate(rows, axis=0).astype(BF16)
        part = pl.ds(80 * step, 80)
        stores.append(pltpu.make_async_copy(out.at[:, part], out_hbm.at[:, part], go.at[step]))
        stores[-1].start()
    for copy in stores:
        copy.wait()


def parts_kernel(place_ref, in_ref, *out_refs):
    for d, out_ref in enumerate(out_refs):
        out_ref[...] = in_ref[pl.ds(pl.multiple_of((place_ref[0] + d) % 4 * 400, 16), 400), :]


def total_kernel(a_ref, b_ref, c_ref, d_ref, out_ref, total, split):
    parts = [ref[...].astype(F32) for ref in (a_ref, b_ref, c_ref, d_ref)]
    total[...] = (parts[0] + parts[1]) + (parts[2] + parts[3])
    for j in range(JD):
        v = total[pl.ds(j, SP, stride=JD), :]
        split[pl.ds(j * S, SP, stride=2), :] = v
        split[pl.ds(j * S + 1, SP, stride=2), :] = roll(v, 64)
    for j in range(JD):
        out_ref[j] = split[j * S : (j + 1) * S, 0:64]


def legendre_back_kernel(seeds_hbm, masked_hbm, out_ref, three, out, seeds, masked, come, come2):
    copies, later = [], []
    for step in range(5):
        part, pairs = pl.ds(80 * step, 80), pl.ds(4 * step, 4)
        copies.append(pltpu.make_async_copy(seeds_hbm.at[:, part], seeds.at[:, part], come.at[step]))
        later.append(pltpu.make_async_copy(masked_hbm.at[pairs], masked.at[pairs], come2.at[step]))
        copies[-1].start()
        later[-1].start()
    three[...] = jnp.zeros_like(three)
    low = lanes(L) < 64
    for step in range(5):
        copies[step].wait()
        later[step].wait()
        values = [seeds[n, 80 * step : 80 * step + 80, :].astype(F32) for n in range(32)]
        for g in (2 * step, 2 * step + 1):
            at = g % 2 * 40
            even = jnp.concatenate([v[at : at + 24] for v in values], axis=0).astype(BF16)
            odd = jnp.concatenate([v[at + 16 : at + 40] for v in values], axis=0).astype(BF16)
            right = jnp.concatenate([even, odd], axis=1)
            left = jnp.concatenate([masked[2 * g], masked[2 * g + 1]], axis=0)
            result = dot(left, right, 1, 0)
            for t in range(2):
                p = 2 * g + t
                both = result[80 * t : 80 * t + 80, 128 * t : 128 * t + 128]
                three[p // 3, p % 3 * L : p % 3 * L + L, :] = jnp.where(low, both[0:L], both[L : 2 * L])
    for p3 in range(7):
        v = three[p3].T
        for row in range(8):
            out[pl.ds(p3 * 8 + row, Z, stride=WR), :] = v[row * Z : row * Z + Z]
    for d in range(Z):
        out_ref[d] = out[d * WR : (d + 1) * WR, :].astype(BF16)


def fourier_back_kernel(in_hbm, table_ref, out_ref, got, waves, rests, out, in_ref, sem):
    fetch(in_hbm, in_ref, sem)
    for d in range(Z):
        got[d * WR : (d + 1) * WR, :] = in_ref[d].astype(F32)
    lane = lanes(Z)

    def piece(q, c2):
        row, place = wave_piece(q, c2)
        return roll(got[pl.ds(row, Z, stride=WR), :], 40 * (c2 - place))

    for i in range(8):
        p, m = (i % 4, i // 4) if i % 4 == 0 else (min(i, 8 - i), int(i > 4))
        for r in range(2):
            for b in range(BB):
                q = (i * 2 + r) * BB + b
                v = jnp.where(lane < 40, piece(q, 0), piece(q, 1))
                v = jnp.where(lane < 80, v, 0.0)
                at = p * 384 + (m * 2 + r) * NB + b * Z
                waves[at : at + Z, :] = v
    pairs = []
    for p in range(4):
        waves[p * 384 + 320 : p * 384 + 384, :] = jnp.zeros((64, 128), F32)
        left = jnp.concatenate(
            [waves[p * 384 + 128 * t : p * 384 + 128 * t + 128, :].T for t in range(3)], axis=1
        )
        left = left[0:80, 0:320].astype(BF16)
        pairs.append(dot(left, table_ref[p], 1, 0))
    for h in range(2):
        mains = [(v[:, 128 * h : 128 * h + 128], v[:, 256 + 128 * h : 384 + 128 * h]) for v in pairs]
        for p, v in enumerate(eight_back(mains)):
            out[(2 * p + h) * GR : (2 * p + h) * GR + 80, :] = v
    lane = lanes(20)
    for p in range(4):
        rests[p * 80 : p * 80 + 80, :] = pairs[p][:, 512:640]
    for h in range(2):
        packed = []
        for p in range(4):
            halves = []
            for part in range(2):
                pos = part * 2 + h
                v = None
                for e in range(4):
                    at = p * 80 + 10 * e
                    rows = jnp.concatenate([rests[at : at + 10, :], rests[at + 40 : at + 50, :]], axis=0)
                    rows = roll(rows, 32 * (e - pos))
                    v = rows if v is None else jnp.where(lane >= 32 * e, rows, v)
                halves.append(v)
            packed.append(tuple(halves))
        for p, v in enumerate(eight_back(packed)):
            out[(2 * p + h) * GR + 80 : (2 * p + h) * GR + 100, :] = v
    for d in range(Z):
        out_ref[d] = out[d * GR : (d + 1) * GR, :].astype(BF16)


def prep_basis(own, basis):
    return call(
        prep_basis_kernel,
        "prep_basis",
        (shape((SP, 2 * L, JW)), shape((SP, JW, 128))),
        [
            pltpu.VMEM((5, L * S, 128), F32),
            pltpu.VMEM((2, 5, 128, 128), F32),
            pltpu.VMEM((2, J, 128), F32),
            pltpu.VMEM((2, JW, 128), F32),
        ],
        smem=1,
        vmem=VMEM_ALL,
    )(own, basis)


def prep_table(block_slot):
    slots = jnp.arange(NB, dtype=jnp.int32)
    holder = jnp.sum(jnp.where(block_slot[None, :] == slots[:, None], slots[None, :], 0), axis=1)
    holder = holder.astype(jnp.int32)
    lane = np.arange(128)
    k = np.concatenate((lane, 160 + lane, 160 * (lane % 64 // 32) + 128 + lane % 32)).astype(np.int32)
    order = holder.reshape(Z, BB).T.reshape(NB)
    phase = (order[:, None] * k[None, :]) % 320
    angle = phase.astype(F32) * (2.0 * math.pi / 320)
    fine = 2.0 * math.pi * np.arange(8)[:, None] * k[None, :] / NLON
    scale = 1.0 / math.sqrt(NLON)
    ci = jnp.asarray((np.cos(fine) * scale).astype(np.float32))
    si = jnp.asarray((np.sin(fine) * scale).astype(np.float32))
    table = call(
        prep_table_kernel, "prep_table", shape((4, 320, 640)), []
    )(jnp.cos(angle), jnp.sin(angle), ci, si)
    return holder, table


def column_step(fields, weight_in, weight_out_t, seeds):
    return call(
        column_kernel,
        "column",
        (shape((Z, GR, 128)), shape((C, L * K)), shape((JD * SP, 128))),
        [
            pltpu.VMEM((C * L, 128), F32),
            pltpu.VMEM((C * L, 128), F32),
            pltpu.VMEM((Z * GR, 128), F32),
            pltpu.VMEM((JD * S, 128), F32),
            pltpu.VMEM((JD * SP, 128), F32),
        ],
        vmem=VMEM_ALL,
    )(fields, weight_in, weight_out_t, seeds)


def column_back(keep, chunks, weight_in, weight_out_t):
    return call(
        column_back_kernel,
        "column_back",
        shape((C, L, K)),
        [
            pltpu.VMEM((C * L, 128), F32),
            pltpu.VMEM((C * L, 128), F32),
            pltpu.VMEM((Z * GR, 128), F32),
            pltpu.VMEM((C, 640), F32),
            *fetched(Z, GR, 128),
        ],
        hbm=(1,),
    )(keep, chunks, weight_in, weight_out_t)


def fourier(chunks, table):
    return call(
        fourier_kernel,
        "fourier",
        shape((Z, WR, 128)),
        [
            pltpu.VMEM((Z * GR, 128), F32),
            pltpu.VMEM((80, 128), F32),
            pltpu.VMEM((2 * M, 128), F32),
            pltpu.VMEM((Z * WR, 128), F32),
            *fetched(Z, GR, 128),
        ],
        hbm=(0,),
    )(chunks, table)


def fourier_back(chunks, table):
    return call(
        fourier_back_kernel,
        "fourier_back",
        shape((Z, GR, 128)),
        [
            pltpu.VMEM((Z * WR, 128), F32),
            pltpu.VMEM((4 * 384, 128), F32),
            pltpu.VMEM((320, 128), F32),
            pltpu.VMEM((Z * GR, 128), F32),
            *fetched(Z, WR, 128),
        ],
        hbm=(0,),
    )(chunks, table)


def legendre(chunks, turned):
    return call(
        legendre_kernel,
        "legendre",
        shape((32, JD * SP, 128)),
        [
            pltpu.VMEM((Z * WR, 128), F32),
            pltpu.VMEM((7, 128, 128), F32),
            pltpu.VMEM((S // 4, 256, 256), BF16),
            pltpu.VMEM((SP, JW, 128), BF16),
            pltpu.VMEM((32, JD * SP, 128), BF16),
            pltpu.SemaphoreType.DMA((5,)),
            pltpu.SemaphoreType.DMA((5,)),
            *fetched(Z, WR, 128),
        ],
        hbm=(0, 1),
        out_hbm=True,
        vmem=VMEM_ALL,
    )(chunks, turned)


def chip_parts(place, sums):
    return call(parts_kernel, "chip_parts", (shape((400, 128)),) * 4, [], smem=1)(place, sums)


def total(parts):
    return call(
        total_kernel,
        "total",
        shape((JD, S, 2 * C), F32),
        [pltpu.VMEM((JD * SP, 128), F32), pltpu.VMEM((JD * S, 128), F32)],
    )(*parts)


def legendre_back(seeds, masked):
    return call(
        legendre_back_kernel,
        "legendre_back",
        shape((Z, WR, 128)),
        [
            pltpu.VMEM((7, 128, 128), F32),
            pltpu.VMEM((Z * WR, 128), F32),
            pltpu.VMEM((32, JD * SP, 128), BF16),
            pltpu.VMEM((SP, 2 * L, JW), BF16),
            pltpu.SemaphoreType.DMA((5,)),
            pltpu.SemaphoreType.DMA((5,)),
        ],
        hbm=(0, 1),
        vmem=VMEM_ALL,
    )(seeds.reshape(32, JD * SP, 128), masked)


def exchange(values):
    return lax.all_to_all(values, "lon", split_axis=0, concat_axis=0, tiled=True)


def position(axis):
    return lax.axis_index(axis).astype(jnp.int32).reshape(1)


def after(values, earlier):
    return lax.optimization_barrier((values, earlier))[0]


def along(parts, axis):
    return [parts[0]] + [
        lax.ppermute(parts[d], axis, [(i, (i + d) % 4) for i in range(4)]) for d in (2, 1, 3)
    ]


def local(grid_fields, weight_in, weight_out, legendre_basis, block_slot, spectrum_grad):
    weight_out_t = weight_out.T
    chunks, keep, seeds = column_step(grid_fields, weight_in, weight_out_t, spectrum_grad)
    seeds = lax.all_gather(seeds, ("y", "x", "core"), axis=0, tiled=True)
    chunks, block_slot, legendre_basis = lax.optimization_barrier((chunks, block_slot, legendre_basis))
    chunks = exchange(chunks)
    holder, table = prep_table(block_slot)
    own = lax.dynamic_slice_in_dim(holder, lax.axis_index("lon") * BB, BB)
    masked, turned = prep_basis(own, legendre_basis)
    waves = exchange(fourier(chunks, table))
    sums = legendre(waves, turned)
    back = legendre_back(seeds, after(masked, sums))
    sums = lax.psum_scatter(sums.reshape(J * SP, 128), ("x", "core"), scatter_dimension=0, tiled=True)
    chunks = fourier_back(exchange(back), table)
    parts = along(chip_parts(position("y"), after(sums, chunks)), "y")
    spectrum = total(parts)
    fields_grad = column_back(keep, after(exchange(chunks), spectrum), weight_in, weight_out_t)
    return (spectrum, fields_grad)


def solution(mesh):
    split = Mesh(mesh.devices.reshape(4, 4, 2, Z), ("y", "x", "core", "lon"))
    lat = ("y", "x", "core")
    in_specs = (P(None, lat, "lon"), P(), P(), P(lat, "lon", None), P(), P(lat, "lon", None))
    out_specs = (P(lat, "lon", None), P(None, lat, "lon"))
    return jax.shard_map(local, mesh=split, in_specs=in_specs, out_specs=out_specs, check_vma=False)
```
